128 devices in a mesh: gx: 16 (over y_hi, x, core), gy: 8 (over y_lo, z).
Axes of the slice: x: 4, y: 4 (y_hi: 2, y_lo: 2; y = y_hi * 2 + y_lo), z: 4, core: 2. Of those that a mesh axis runs over, the one named last changes fastest.
Arguments:
- air_vector: float32 [128, 256, 2048], P(None, 'gx', 'gy'), may hold values from -6 to 6
- sea_vector: float32 [64, 128, 4096], P(None, 'gx', 'gy'), may hold values from -6 to 6
- air_scaling: float32 [128, 256, 2048], P(None, 'gx', 'gy'), may hold values from 0.5 to 2
- sea_scaling: float32 [64, 128, 4096], P(None, 'gx', 'gy'), may hold values from 0.5 to 2
- air_weights: float32 [128, 256, 2048], P(None, 'gx', 'gy'), may hold values from 0.3 to 3
- sea_weights: float32 [64, 128, 4096], P(None, 'gx', 'gy'), may hold values from 0.3 to 3
- air_column: float32 [128, 128], replicated, may hold values from -0.5 to 0.5
- sea_column: float32 [64, 64], replicated, may hold values from -0.75 to 0.75
- land_mask: int32 [128, 4096], P('gx', 'gy'), may hold values 0 or 1
- flux_index: int32 [8, 512, 4], P('gy', 'gx'), may hold values from 0 to 511, as said below
- flux_count: int32 [8, 512], P('gy', 'gx'), may hold values from 1 to 4
- flux_tiles: bfloat16 [8, 512, 4, 128, 128], P('gy', 'gx'), may hold values from -0.25 to 0.25
- skin_index: int32 [8, 512, 4], P('gy', 'gx'), may hold values from 0 to 511, as said below
- skin_count: int32 [8, 512], P('gy', 'gx'), may hold values from 1 to 4
- skin_tiles: bfloat16 [8, 512, 4, 128, 128], P('gy', 'gx'), may hold values from -0.25 to 0.25
Outputs:
- air_gradient: float32 [128, 256, 2048], P(None, 'gx', 'gy')
- sea_gradient: float32 [64, 128, 4096], P(None, 'gx', 'gy')
The draws below stay inside these ranges and needn't reach their ends.
Inputs may be any that keep to these rules, and one draw needn't show every extreme that they name: `flux_index`: slot 0 names the atmosphere block with the same number as the ocean block; every other slot names that block or one beside it in the tile row (block 511 lies beside block 0); slots at or past the count are padding and are not used. `skin_index`: slot 0 names the ocean block with the same number as the atmosphere block; every other slot names that block or one beside it in the tile row (block 511 lies beside block 0); slots at or past the count are padding and are not used.
All inputs are finite; a program needn't handle non-finite values. No bound on the sum of `land_mask` on one device may be relied on, other than what follows from the above.
Results may differ from the reference program's by a relative error of at most 0.00069.
Values may be sent and summed in bfloat16 or wider, within the bound.
A program may use at most 128 MiB of HBM per device.

```python
import math
import jax
import jax.numpy as jnp
from jax import lax

AIR_LEVELS = 128
SEA_LEVELS = 64
FIELDS = 4
BLOCK = 128
SLOTS = 4
AIR_X = 16
AIR_Y = 256
SEA_X = 8
SEA_Y = 512
AIR_ROW = 512
SEA_ROW = 512
AIR_LON = 256
AIR_LAT = 2048
SEA_LON = 128
SEA_LAT = 4096
N_GX = 16
N_GY = 8


def intersection_places(key, row_length, slots):
    offsets = jax.random.randint(key, (N_GY, row_length, slots), -1, 2).astype(jnp.int32)
    offsets = offsets.at[:, :, 0].set(0)
    own_block = jnp.arange(row_length, dtype=jnp.int32)[None, :, None]
    return ((own_block + offsets) % row_length).astype(jnp.int32)


def draw_flux_index(key, part):
    key = jax.random.fold_in(key, 11)
    return intersection_places(key, SEA_ROW, SLOTS)


def draw_skin_index(key, part):
    key = jax.random.fold_in(key, 23)
    return intersection_places(key, AIR_ROW, SLOTS)


def touch_ends(result, key, least, top_value):
    index_at = [jax.random.randint(jax.random.fold_in(key, axis), (), 0, length) for axis, length in enumerate(result.shape)]
    widest = result.shape.index(max(result.shape))
    neighbour = index_at[:widest] + [(index_at[widest] + 1) % result.shape[widest]] + index_at[widest + 1:]
    return result.at[tuple(index_at)].set(least).at[tuple(neighbour)].set(top_value)


def steps_of(key, shape, pieces, low, high):
    def one(position, shards_of):
        heights = jax.random.uniform(jax.random.fold_in(jax.random.fold_in(key, 6), position), (shards_of,), jnp.float32, low / len(pieces), high / len(pieces))
        return jnp.repeat(jnp.exp(heights), shape[position] // shards_of).reshape((-1,) + (1,) * (len(shape) - position - 1))

    loudness = one(*pieces[0])
    for cut in pieces[1:]:
        loudness = loudness * one(*cut)
    return loudness


def scatter_about(rng, dims, spread, bound, split=(), held_as=jnp.bfloat16):
    drawn = jax.random.normal(rng, dims, jnp.float32) * spread
    if len(split) > 0:
        drawn = steps_of(rng, dims, split, -0.22, 0.18) * drawn
    return jnp.clip(drawn, min=-bound, max=bound).astype(held_as)


def setup_inputs(seed: int = 0) -> dict:
    streams_of = jax.random.split(jax.random.key(seed), 16)
    air_vector = scatter_about(streams_of[0], (AIR_LEVELS, AIR_LON, AIR_LAT), 1.0, 6.0, ((1, 16), (2, 8)), jnp.float32)
    sea_vector = scatter_about(streams_of[1], (SEA_LEVELS, SEA_LON, SEA_LAT), 1.0, 6.0, ((1, 16), (2, 8)), jnp.float32)
    air_scaling = jnp.clip(jnp.exp(math.log(2.0) - 1.3862944 * jax.random.uniform(streams_of[2], (AIR_LEVELS, AIR_LON, AIR_LAT), jnp.float32) ** steps_of(streams_of[2], (AIR_LEVELS, AIR_LON, AIR_LAT), ((1, 16), (2, 8)), -0.2, 0.2)), 0.5, 2.0)
    sea_scaling = jnp.clip(jnp.exp(math.log(2.0) - 1.3862944 * jax.random.uniform(streams_of[3], (SEA_LEVELS, SEA_LON, SEA_LAT), jnp.float32) ** steps_of(streams_of[3], (SEA_LEVELS, SEA_LON, SEA_LAT), ((1, 16), (2, 8)), -0.2, 0.2)), 0.5, 2.0)
    air_weights = jnp.clip(jnp.exp(math.log(3.0) - 2.3025851 * jax.random.uniform(streams_of[4], (AIR_LEVELS, AIR_LON, AIR_LAT), jnp.float32) ** steps_of(streams_of[4], (AIR_LEVELS, AIR_LON, AIR_LAT), ((1, 16), (2, 8)), -0.2, 0.2)), 0.3, 3.0)
    sea_weights = jnp.clip(jnp.exp(math.log(3.0) - 2.3025851 * jax.random.uniform(streams_of[5], (SEA_LEVELS, SEA_LON, SEA_LAT), jnp.float32) ** steps_of(streams_of[5], (SEA_LEVELS, SEA_LON, SEA_LAT), ((1, 16), (2, 8)), -0.2, 0.2)), 0.3, 3.0)
    air_column = scatter_about(streams_of[6], (AIR_LEVELS, AIR_LEVELS), AIR_LEVELS ** -0.5, 0.5, (), jnp.float32)
    sea_column = scatter_about(streams_of[7], (SEA_LEVELS, SEA_LEVELS), SEA_LEVELS ** -0.5, 0.75, (), jnp.float32)
    land_mask = touch_ends((jax.random.randint(streams_of[8], (SEA_LON, SEA_LAT), 0, 10) < 7).astype(jnp.int32), jax.random.fold_in(streams_of[8], 1), 0, 1)
    flux_index = draw_flux_index(jax.random.fold_in(streams_of[15], 71), 0)
    flux_count = touch_ends(jax.random.randint(streams_of[10], (N_GY, SEA_ROW), 1, SLOTS + 1), jax.random.fold_in(streams_of[10], 1), 1, SLOTS).astype(jnp.int32)
    flux_tiles = scatter_about(streams_of[11], (N_GY, SEA_ROW, SLOTS, BLOCK, BLOCK), (SLOTS * BLOCK) ** -0.5, 0.25, ((0, 8), (1, 16)))
    skin_index = draw_skin_index(jax.random.fold_in(streams_of[15], 71), 0)
    skin_count = touch_ends(jax.random.randint(streams_of[13], (N_GY, AIR_ROW), 1, SLOTS + 1), jax.random.fold_in(streams_of[13], 1), 1, SLOTS).astype(jnp.int32)
    skin_tiles = scatter_about(streams_of[14], (N_GY, AIR_ROW, SLOTS, BLOCK, BLOCK), (SLOTS * BLOCK) ** -0.5, 0.25, ((0, 8), (1, 16)))
    return {"air_vector": air_vector, "sea_vector": sea_vector, "air_scaling": air_scaling, "sea_scaling": sea_scaling, "air_weights": air_weights, "sea_weights": sea_weights, "air_column": air_column, "sea_column": sea_column, "land_mask": land_mask, "flux_index": flux_index, "flux_count": flux_count, "flux_tiles": flux_tiles, "skin_index": skin_index, "skin_count": skin_count, "skin_tiles": skin_tiles}


lap_gain = 0.2


def laplace(grid_field):
    east_west = jnp.roll(grid_field, 1, axis=1) + jnp.roll(grid_field, -1, axis=1)
    padded = jnp.pad(grid_field, ((0, 0), (0, 0), (1, 1)))
    north_south = padded[:, :, 2:] + padded[:, :, :-2]
    return east_west + north_south - 4.0 * grid_field


def columns(matrix, grid_field):
    levels = grid_field.shape[0]
    flat_field = grid_field.reshape(levels, -1)
    product = jnp.dot(matrix, flat_field, precision=lax.Precision.HIGHEST, preferred_element_type=jnp.float32)
    return product.reshape(grid_field.shape)


def to_blocks(surface, tile_x, tile_y):
    fields = surface.shape[0]
    shaped = surface.reshape(fields, N_GX, tile_x, N_GY, tile_y).transpose(3, 0, 1, 2, 4)
    return shaped.reshape(N_GY, fields, N_GX * tile_x * tile_y // BLOCK, BLOCK)


def from_blocks(blocks, tile_x, tile_y):
    fields = blocks.shape[1]
    shaped = blocks.reshape(N_GY, fields, N_GX, tile_x, tile_y).transpose(1, 2, 3, 0, 4)
    return shaped.reshape(fields, N_GX * tile_x, N_GY * tile_y)


def slot_mask(slot_count, slots):
    return jnp.arange(slots)[None, :] < slot_count[:, None]


def regrid_forward(source_blocks, slot_index, slot_count, slot_tiles):
    def one_row(packed):
        row_source, row_index, row_count, row_tiles = packed
        picked = jnp.take(row_source, row_index, axis=1)
        in_use = slot_mask(row_count, row_index.shape[1])
        picked = jnp.where(in_use[None, :, :, None], picked, jnp.zeros((), picked.dtype))
        return jnp.einsum("okij,fokj->foi", row_tiles.astype(jnp.float32), picked.astype(jnp.float32),
                          precision=lax.Precision.HIGHEST)
    return lax.map(one_row, (source_blocks, slot_index, slot_count, slot_tiles))


def regrid_back(adjoint_blocks, slot_index, slot_count, slot_tiles, row_length):
    def one_row(packed):
        row_adjoint, row_index, row_count, row_tiles = packed
        contributions = jnp.einsum("okij,foi->okfj", row_tiles.astype(jnp.float32), row_adjoint.astype(jnp.float32),
                                   precision=lax.Precision.HIGHEST)
        in_use = slot_mask(row_count, row_index.shape[1])
        contributions = jnp.where(in_use[:, :, None, None], contributions, jnp.zeros((), contributions.dtype))
        fields = contributions.shape[2]
        summed = jax.ops.segment_sum(contributions.reshape(-1, fields, BLOCK), row_index.reshape(-1),
                                     num_segments=row_length)
        return summed.transpose(1, 0, 2)
    return lax.map(one_row, (adjoint_blocks, slot_index, slot_count, slot_tiles))


def reference(air_vector, sea_vector, air_scaling, sea_scaling, air_weights, sea_weights, air_column, sea_column,
              land_mask, flux_index, flux_count, flux_tiles, skin_index, skin_count, skin_tiles):
    sea_mask = land_mask.astype(jnp.float32)[None]
    low_pad = ((AIR_LEVELS - FIELDS, 0), (0, 0), (0, 0))
    top_pad = ((0, SEA_LEVELS - FIELDS), (0, 0), (0, 0))
    air_one = air_vector + lap_gain * laplace(air_vector)
    air_two = columns(air_column, air_scaling * air_one)
    sea_zero = sea_mask * sea_vector
    sea_one = sea_zero + lap_gain * sea_mask * laplace(sea_zero)
    air_surface = to_blocks(air_two[AIR_LEVELS - FIELDS:].astype(jnp.bfloat16), AIR_X, AIR_Y)
    sea_surface = to_blocks(sea_one[:FIELDS].astype(jnp.bfloat16), SEA_X, SEA_Y)
    flux_sea = from_blocks(regrid_forward(air_surface, flux_index, flux_count, flux_tiles), SEA_X, SEA_Y)
    skin_air = from_blocks(regrid_forward(sea_surface, skin_index, skin_count, skin_tiles), AIR_X, AIR_Y)
    sea_two = sea_one + sea_mask * jnp.pad(flux_sea, top_pad)
    sea_three = sea_mask * columns(sea_column, sea_scaling * sea_two)
    air_three = air_two + jnp.pad(skin_air, low_pad)
    air_forcing = air_weights * air_three
    sea_forcing = sea_weights * sea_three
    sea_adjoint = sea_scaling * columns(sea_column.T, sea_mask * sea_forcing)
    flux_adjoint = to_blocks((sea_mask * sea_adjoint)[:FIELDS].astype(jnp.bfloat16), SEA_X, SEA_Y)
    skin_adjoint = to_blocks(air_forcing[AIR_LEVELS - FIELDS:].astype(jnp.bfloat16), AIR_X, AIR_Y)
    flux_back = from_blocks(regrid_back(flux_adjoint, flux_index, flux_count, flux_tiles, AIR_ROW), AIR_X, AIR_Y)
    skin_back = from_blocks(regrid_back(skin_adjoint, skin_index, skin_count, skin_tiles, SEA_ROW), SEA_X, SEA_Y)
    sea_upper = sea_adjoint + jnp.pad(skin_back, top_pad)
    sea_gradient = sea_mask * (sea_upper + lap_gain * laplace(sea_mask * sea_upper))
    air_lower = air_forcing + jnp.pad(flux_back, low_pad)
    air_upper = air_scaling * columns(air_column.T, air_lower)
    air_gradient = air_upper + lap_gain * laplace(air_upper)
    return (air_gradient, sea_gradient)
```

```python
import functools

import jax
import jax.numpy as jnp
from jax import lax
from jax.experimental import pallas as pl
from jax.experimental.pallas import tpu as pltpu
from jax.sharding import PartitionSpec as P

FIELDS = 4
GAIN = 0.2
MESH = pl.DeviceIdType.MESH
f32, bf16 = jnp.float32, jnp.bfloat16


def split_cat(w):
    hi = w.astype(bf16)
    lo = (w - hi.astype(f32)).astype(bf16)
    return jnp.concatenate(
        [jnp.concatenate([hi, hi], axis=1), jnp.concatenate([lo, lo], axis=1)], axis=0
    )


def col(cat, field):
    n = field.shape[0]
    hi = field.astype(bf16)
    lo = (field - hi.astype(f32)).astype(bf16)
    r = jnp.dot(cat, jnp.concatenate([hi, lo], axis=0), preferred_element_type=f32)
    return r[:n] + r[n:]


def rounded(v):
    return v.astype(bf16).astype(f32)


def lane_shifts(v, lo, hi):
    n = v.shape[1]
    lane = lax.broadcasted_iota(jnp.int32, v.shape, 1)
    down = jnp.where(lane == 0, lo, pltpu.roll(v, 1, 1))
    up = jnp.where(lane == n - 1, hi, pltpu.roll(v, n - 1, 1))
    return down + up


def row_iota():
    return lax.broadcasted_iota(jnp.int32, (8, 128), 0)


def kernel(
    nx, ny, air_x, sea_x,
    av, sv, asc, ssc, aw, sw, wa, wo, mask, fidx, fcnt, ftil, sidx, scnt, stil,
    aout, sout,
    av_s, sv_s, as_s, ss_s, aw_s, sw_s, wa_s, wo_s, mask_s, fidx_s, fcnt_s, ft_s, sidx_s, scnt_s, st_s,
    wcat, wcat_t, ocat, ocat_t, mf,
    at, s1, adj, au, so, ao,
    dx_f, dx_s, S_a, S_o, L_f, L_s, F, G, A_f, A_s, Cf, Cs, R_f, R_s,
    xl_a, xr_a, xl_o, xr_o, e_lo, e_hi, h_lo, h_hi,
    xl2_a, xr2_a, xl2_o, xr2_o, e2_lo, e2_hi, h2_lo, h2_hi,
    in_sem, out_sem, send_sem, recv_sem,
):
    gx, gy = lax.axis_index("gx"), lax.axis_index("gy")
    right, left = lax.rem(gx + 1, nx), lax.rem(gx + nx - 1, nx)
    above, below = lax.rem(gy + 1, ny), lax.rem(gy + ny - 1, ny)
    to_right, to_left = (right, gy), (left, gy)
    to_above, to_below = (gx, above), (gx, below)

    def load_columns(src, dst, sem, count):
        for x in range(count):
            pltpu.make_async_copy(src.at[:, x, :], dst.at[x], in_sem.at[sem]).start()

    def loaded(dst, sem):
        pltpu.make_async_copy(dst, dst, in_sem.at[sem]).wait()

    def load(src, dst, sem):
        pltpu.make_async_copy(src, dst, in_sem.at[sem]).start()

    barrier = pltpu.get_barrier_semaphore()
    for device in (to_right, to_left, to_above, to_below):
        pl.semaphore_signal(barrier, inc=1, device_id=device, device_id_type=MESH)

    load(mask, mask_s, 0)
    load_columns(sv, sv_s, 1, sea_x)
    load_columns(av, av_s, 2, air_x)
    load(wa, wa_s, 3)
    load(wo, wo_s, 4)
    load(fidx.at[0], fidx_s, 5)
    load(fcnt, fcnt_s, 6)
    load(sidx.at[0], sidx_s, 7)
    load(scnt, scnt_s, 8)
    load_columns(asc, as_s, 9, air_x)
    load(ftil.at[0], ft_s, 10)
    load(stil.at[0], st_s, 11)
    load_columns(ssc, ss_s, 12, sea_x)
    load_columns(sw, sw_s, 13, sea_x)
    load_columns(aw, aw_s, 14, air_x)

    pl.semaphore_wait(barrier, 4)

    def remote(src, dst, k, device):
        return pltpu.make_async_remote_copy(
            src_ref=src, dst_ref=dst, send_sem=send_sem.at[k], recv_sem=recv_sem.at[k],
            device_id=device, device_id_type=MESH,
        )

    halo_xr = remote(av.at[:, air_x - 1, :], xl_a, 0, to_right)
    halo_xl = remote(av.at[:, 0, :], xr_a, 1, to_left)
    halo_xr.start()
    halo_xl.start()

    loaded(mask_s, 0)
    mf[...] = mask_s[...].astype(f32)
    loaded(sv_s, 1)

    lane64 = lax.broadcasted_iota(jnp.int32, (64, 128), 1)
    zero64 = jnp.zeros((64, 128), f32)

    def sea_zero(x, acc):
        lo, hi = acc
        z = mf[pl.ds(x, 1), :] * sv_s[x]
        sv_s[x] = z
        here = lane64 == x + 2 * air_x
        lo = jnp.where(here, z[:, 0:1], lo)
        hi = jnp.where(here, z[:, -1:], hi)
        return lo, hi

    edges = lax.fori_loop(0, sea_x, sea_zero, (zero64, zero64))
    halo_or = remote(sv_s.at[sea_x - 1], xl_o, 2, to_right)
    halo_ol = remote(sv_s.at[0], xr_o, 3, to_left)
    halo_or.start()
    halo_ol.start()

    loaded(av_s, 2)

    def pack_air(field, x, acc):
        lo, hi = acc
        for part in range(2):
            v = field[64 * part:64 * part + 64]
            here = lane64 == x + part * air_x
            lo = jnp.where(here, v[:, 0:1], lo)
            hi = jnp.where(here, v[:, -1:], hi)
        return lo, hi

    edges = lax.fori_loop(0, air_x, lambda x, acc: pack_air(av_s[x], x, acc), edges)
    e_lo[...], e_hi[...] = edges
    halo_yu = remote(e_hi, h_lo, 4, to_above)
    halo_yd = remote(e_lo, h_hi, 5, to_below)
    halo_yu.start()
    halo_yd.start()

    loaded(wa_s, 3)
    loaded(wo_s, 4)
    wcat[...] = split_cat(wa_s[...])
    wcat_t[...] = split_cat(wa_s[...].T)
    ocat[...] = split_cat(wo_s[...])
    ocat_t[...] = split_cat(wo_s[...].T)

    row_blocks = 32 * nx

    def places(idx_s, cnt_s, dx):
        own = gx * 32 + lax.broadcasted_iota(jnp.int32, (4, 32), 1)
        rel = idx_s[...] - own
        d = jnp.where(rel == 0, 0.0, jnp.where((rel == 1) | (rel == 1 - row_blocks), 1.0, -1.0))
        block = lax.broadcasted_iota(jnp.int32, (128, 32), 0) // 4
        pick = jnp.where(block == lax.broadcasted_iota(jnp.int32, (128, 32), 1), 1.0, 0.0)
        count = cnt_s[...].astype(f32)
        for k in range(4):
            dk = jnp.where(count > k, d[k:k + 1, :], 2.0)
            dx[k] = jnp.broadcast_to(jnp.sum(pick * dk, axis=1, keepdims=True), (128, 128))

    loaded(fidx_s, 5)
    loaded(fcnt_s, 6)
    places(fidx_s, fcnt_s, dx_f)
    loaded(sidx_s, 7)
    loaded(scnt_s, 8)
    places(sidx_s, scnt_s, dx_s)

    halo_xl.wait()
    halo_xr.wait()
    halo_ol.wait()
    halo_or.wait()
    halo_yu.wait()
    halo_yd.wait()

    def zero_outside(h):
        lo = jnp.where(gy == 0, 0.0, h[0][...])
        hi = jnp.where(gy == ny - 1, 0.0, h[1][...])
        h[0][...] = lo
        h[1][...] = hi

    zero_outside((h_lo, h_hi))

    def pick_lane(packed, lane):
        return jnp.sum(jnp.where(lane64 == lane, packed, 0.0), axis=1, keepdims=True)

    def air_ends(hl, hh, x):
        lo = jnp.concatenate([pick_lane(hl[...], x), pick_lane(hl[...], x + air_x)], axis=0)
        hi = jnp.concatenate([pick_lane(hh[...], x), pick_lane(hh[...], x + air_x)], axis=0)
        return lo, hi

    def sea_ends(hl, hh, x):
        return pick_lane(hl[...], x + 2 * air_x), pick_lane(hh[...], x + 2 * air_x)

    loaded(as_s, 9)
    half = row_iota() < 4

    def air_first(x, west, east):
        v = av_s[x]
        lo, hi = air_ends(h_lo, h_hi, x)
        one = GAIN * (v + west + east + lane_shifts(v, lo, hi))
        two = col(wcat[...], as_s[x] * one)
        at[x] = two
        low = rounded(two[120:128])
        slab = jnp.where(half, pltpu.roll(low[:, 0:128], 4, 0), low[:, 128:256])
        S_a[pl.ds(pl.multiple_of(8 + 8 * x, 8), 8), :] = slab

    air_first(0, xl_a[...], av_s[1])
    air_first(air_x - 1, av_s[air_x - 2], xr_a[...])

    def send_rims(src_hi, src_lo, dst_hi, dst_lo, k):
        up = remote(src_hi.at[128:136], dst_hi.at[0:8], k, to_right)
        down = remote(src_lo.at[8:16], dst_lo.at[136:144], k + 1, to_left)
        up.start()
        down.start()
        return up, down

    rim_a = send_rims(S_a, S_a, S_a, S_a, 6)

    def sea_first(x, west, east):
        v = sv_s[x]
        m = mf[pl.ds(x, 1), :]
        lo, hi = sea_ends(h_lo, h_hi, x)
        one = v + (GAIN * m) * (west + east + lane_shifts(v, lo, hi) - 4.0 * v)
        s1[x] = one
        top = rounded(one[0:8])
        for q in range(2):
            a = top[:, 256 * q:256 * q + 128]
            b = top[:, 256 * q + 128:256 * q + 256]
            slab = jnp.where(half, a, pltpu.roll(b, 4, 0))
            S_o[pl.ds(pl.multiple_of(8 + 16 * x + 8 * q, 8), 8), :] = slab

    sea_first(0, xl_o[...], sv_s[1])
    sea_first(sea_x - 1, sv_s[sea_x - 2], xr_o[...])
    rim_o = send_rims(S_o, S_o, S_o, S_o, 8)

    @pl.loop(1, sea_x - 1)
    def _(x):
        sea_first(x, sv_s[x - 1], sv_s[x + 1])

    @pl.loop(1, air_x - 1)
    def _(x):
        air_first(x, av_s[x - 1], av_s[x + 1])

    def gather_rows(S, dx, L, r0, r1):
        s_m, s_0, s_p = S[4 + r0:4 + r1], S[8 + r0:8 + r1], S[12 + r0:12 + r1]
        for k in range(4):
            d = dx[k, r0:r1]
            L[r0:r1, 128 * k:128 * k + 128] = jnp.where(
                d == 0.0, s_0, jnp.where(d == -1.0, s_m, jnp.where(d == 1.0, s_p, 0.0))
            )

    def pair_tiles(T, p):
        return jnp.concatenate(
            [jnp.concatenate([T[2 * p + a, k] for k in range(4)], axis=1) for a in range(2)], axis=0
        )

    def pair_rows(p):
        return pl.ds(pl.multiple_of(8 * p, 8), 8)

    def forward_pair(L, T, out, p):
        r = lax.dot_general(
            L[pair_rows(p), :].astype(bf16), pair_tiles(T, p), (((1,), (1,)), ((), ())),
            preferred_element_type=f32,
        )
        out[pair_rows(p), :] = jnp.where(half, r[:, 0:128], r[:, 128:256])

    def back_pair(A, T, dx, C, p):
        a = A[pair_rows(p), :]
        lhs = jnp.concatenate([jnp.where(half, a, 0.0), jnp.where(half, 0.0, a)], axis=1)
        r = jnp.dot(lhs.astype(bf16), pair_tiles(T, p), preferred_element_type=f32)
        sums = [jnp.zeros((8, 128), f32) for _ in range(3)]
        for k in range(4):
            d = dx[k, pair_rows(p), :]
            c = r[:, 128 * k:128 * k + 128]
            for n in range(3):
                sums[n] = sums[n] + jnp.where(d == n - 1.0, c, 0.0)
        for n in range(3):
            C[n, pl.ds(pl.multiple_of(8 + 8 * p, 8), 8), :] = sums[n]

    gather_rows(S_a, dx_f, L_f, 8, 120)
    gather_rows(S_o, dx_s, L_s, 8, 120)
    loaded(ft_s, 10)
    loaded(st_s, 11)

    @pl.loop(1, 15)
    def _(p):
        forward_pair(L_f, ft_s, F, p)
        forward_pair(L_s, st_s, G, p)

    for c in rim_a + rim_o:
        c.wait()
    for r0 in (0, 120):
        gather_rows(S_a, dx_f, L_f, r0, r0 + 8)
        gather_rows(S_o, dx_s, L_s, r0, r0 + 8)
    for p in (0, 15):
        forward_pair(L_f, ft_s, F, p)
        forward_pair(L_s, st_s, G, p)

    loaded(ss_s, 12)
    loaded(sw_s, 13)

    def sea_top(slabs):
        parts = []
        for slab in slabs:
            parts.append(jnp.where(half, slab, 0.0))
            parts.append(jnp.where(half, pltpu.roll(slab, 4, 0), 0.0))
        return jnp.concatenate(parts, axis=1)

    def sea_slabs(ref, x):
        return [ref[pl.ds(pl.multiple_of(16 * x + 8 * q, 8), 8), :] for q in range(2)]

    def sea_columns(x):
        m = mf[pl.ds(x, 1), :]
        one = s1[x]
        two = jnp.concatenate([one[0:8] + m * sea_top(sea_slabs(F, x)), one[8:]], axis=0)
        three = col(ocat[...], ss_s[x] * two)
        back = ss_s[x] * col(ocat_t[...], m * (sw_s[x] * three))
        adj[x] = back
        top = rounded(m * back[0:8])
        for q in range(2):
            a = top[:, 256 * q:256 * q + 128]
            b = top[:, 256 * q + 128:256 * q + 256]
            A_f[pl.ds(pl.multiple_of(16 * x + 8 * q, 8), 8), :] = jnp.where(half, a, pltpu.roll(b, 4, 0))

    sea_columns(0)
    sea_columns(sea_x - 1)
    for p in (0, 15):
        back_pair(A_f, ft_s, dx_f, Cf, p)
    rim_f = send_rims(Cf.at[2], Cf.at[0], Cf.at[2], Cf.at[0], 10)

    loaded(aw_s, 14)

    def air_low(ref, x):
        slab = ref[pl.ds(pl.multiple_of(8 * x, 8), 8), :]
        return jnp.concatenate(
            [jnp.where(half, 0.0, pltpu.roll(slab, 4, 0)), jnp.where(half, 0.0, slab)], axis=1
        )

    def air_forcing(x):
        two = at[x]
        three = jnp.concatenate([two[0:120], two[120:128] + air_low(G, x)], axis=0)
        forcing = aw_s[x] * three
        at[x] = forcing
        low = rounded(forcing[120:128])
        A_s[pl.ds(pl.multiple_of(8 * x, 8), 8), :] = jnp.where(
            half, pltpu.roll(low[:, 0:128], 4, 0), low[:, 128:256]
        )

    air_forcing(0)
    air_forcing(air_x - 1)
    for p in (0, 15):
        back_pair(A_s, st_s, dx_s, Cs, p)
    rim_s = send_rims(Cs.at[2], Cs.at[0], Cs.at[2], Cs.at[0], 12)

    @pl.loop(1, sea_x - 1)
    def _(x):
        sea_columns(x)

    @pl.loop(1, air_x - 1)
    def _(x):
        air_forcing(x)

    @pl.loop(1, 15)
    def _(p):
        back_pair(A_f, ft_s, dx_f, Cf, p)
        back_pair(A_s, st_s, dx_s, Cs, p)

    for c in rim_f + rim_s:
        c.wait()
    R_f[...] = Cf[1, 8:136] + Cf[0, 12:140] + Cf[2, 4:132]
    R_s[...] = Cs[1, 8:136] + Cs[0, 12:140] + Cs[2, 4:132]

    def sea_upper(x):
        back = adj[x]
        up = jnp.concatenate([back[0:8] + sea_top(sea_slabs(R_s, x)), back[8:]], axis=0)
        z = mf[pl.ds(x, 1), :] * up
        adj[x] = z
        return z

    def air_upper(x):
        low = at[x]
        low = jnp.concatenate([low[0:120], low[120:128] + air_low(R_f, x)], axis=0)
        up = as_s[x] * col(wcat_t[...], low)
        au[x] = up
        return up

    def pack_sea(z, x, acc):
        lo, hi = acc
        here = lane64 == x + 2 * air_x
        return jnp.where(here, z[:, 0:1], lo), jnp.where(here, z[:, -1:], hi)

    edges = (zero64, zero64)
    for x in (0, sea_x - 1):
        edges = pack_sea(sea_upper(x), x, edges)
    for x in (0, air_x - 1):
        edges = pack_air(air_upper(x), x, edges)
    last = [
        remote(au.at[air_x - 1], xl2_a, 14, to_right),
        remote(au.at[0], xr2_a, 15, to_left),
        remote(adj.at[sea_x - 1], xl2_o, 16, to_right),
        remote(adj.at[0], xr2_o, 17, to_left),
    ]
    for c in last:
        c.start()
    edges = lax.fori_loop(1, sea_x - 1, lambda x, acc: pack_sea(sea_upper(x), x, acc), edges)
    edges = lax.fori_loop(1, air_x - 1, lambda x, acc: pack_air(air_upper(x), x, acc), edges)
    e2_lo[...], e2_hi[...] = edges
    last += [remote(e2_hi, h2_lo, 18, to_above), remote(e2_lo, h2_hi, 19, to_below)]
    for c in last[4:]:
        c.start()
    for c in last:
        c.wait()
    zero_outside((h2_lo, h2_hi))

    def sea_last(x, west, east):
        z = adj[x]
        lo, hi = sea_ends(h2_lo, h2_hi, x)
        so[x] = z + (GAIN * mf[pl.ds(x, 1), :]) * (west + east + lane_shifts(z, lo, hi) - 4.0 * z)

    def air_last(x, west, east):
        v = au[x]
        lo, hi = air_ends(h2_lo, h2_hi, x)
        ao[x] = GAIN * (v + west + east + lane_shifts(v, lo, hi))

    sea_last(0, xl2_o[...], adj[1])
    sea_last(sea_x - 1, adj[sea_x - 2], xr2_o[...])

    @pl.loop(1, sea_x - 1)
    def _(x):
        sea_last(x, adj[x - 1], adj[x + 1])

    for x in range(sea_x):
        pltpu.make_async_copy(so.at[x], sout.at[:, x, :], out_sem.at[0]).start()

    air_last(0, xl2_a[...], au[1])
    air_last(air_x - 1, au[air_x - 2], xr2_a[...])

    @pl.loop(1, air_x - 1)
    def _(x):
        air_last(x, au[x - 1], au[x + 1])

    for x in range(air_x):
        pltpu.make_async_copy(ao.at[x], aout.at[:, x, :], out_sem.at[1]).start()
    pltpu.make_async_copy(so, so, out_sem.at[0]).wait()
    pltpu.make_async_copy(ao, ao, out_sem.at[1]).wait()


def shards(*args, nx, ny):
    av, sv = args[0], args[1]
    args = [a.transpose(0, 2, 1) if n in (9, 12) else a for n, a in enumerate(args)]
    levels, air_x, air_y = av.shape
    sea_levels, sea_x, sea_y = sv.shape
    V = pltpu.VMEM
    air = V((air_x, levels, air_y), f32)
    sea = V((sea_x, sea_levels, sea_y), f32)
    blk = V((128, 128), f32)
    ext = V((144, 128), f32)
    rowa, rowo, pack = V((levels, air_y), f32), V((sea_levels, sea_y), f32), V((64, 128), f32)
    tiles = V((32, 4, 128, 128), bf16)
    idx, cnt = V((4, 32), jnp.int32), V((1, 32), jnp.int32)
    wcat = V((2 * levels, 2 * levels), bf16)
    ocat = V((2 * sea_levels, 2 * sea_levels), bf16)
    dx = V((4, 128, 128), f32)
    cterm = V((3, 144, 128), f32)
    dma = pltpu.SemaphoreType.DMA
    scratch = [
        air, sea, air, sea, air, sea, V((levels, levels), f32), V((sea_levels, sea_levels), f32),
        V((sea_x, sea_y), jnp.int32), idx, cnt, tiles, idx, cnt, tiles,
        wcat, wcat, ocat, ocat, V((sea_x, sea_y), f32),
        air, sea, sea, air, sea, air,
        dx, dx, ext, ext, V((128, 512), f32), V((128, 512), f32), blk, blk, blk, blk, cterm, cterm, blk, blk,
        rowa, rowa, rowo, rowo, pack, pack, pack, pack,
        rowa, rowa, rowo, rowo, pack, pack, pack, pack,
        dma((15,)), dma((2,)), dma((20,)), dma((20,)),
    ]
    anywhere = pl.BlockSpec(memory_space=pl.ANY)
    return pl.pallas_call(
        functools.partial(kernel, nx, ny, air_x, sea_x),
        out_shape=(jax.ShapeDtypeStruct(av.shape, f32), jax.ShapeDtypeStruct(sv.shape, f32)),
        in_specs=[anywhere] * 15,
        out_specs=(anywhere, anywhere),
        scratch_shapes=scratch,
        compiler_params=pltpu.CompilerParams(
            collective_id=0, has_side_effects=True, vmem_limit_bytes=56 * 1024 * 1024
        ),
        cost_estimate=pl.CostEstimate(flops=4_000_000_000, bytes_accessed=21_000_000, transcendentals=0),
    )(*args)


def solution(mesh):
    grid = P(None, "gx", "gy")
    index, count, tiles = P("gy", "gx", None), P("gy", "gx"), P("gy", "gx", None, None, None)
    return jax.shard_map(
        functools.partial(shards, nx=mesh.shape["gx"], ny=mesh.shape["gy"]),
        mesh=mesh,
        in_specs=(grid,) * 6 + (P(), P(), P("gx", "gy"), index, count, tiles, index, count, tiles),
        out_specs=(grid, grid),
        check_vma=False,
    )
```

```python
import functools

import jax
import jax.numpy as jnp
from jax import lax
from jax.experimental import pallas as pl
from jax.experimental.pallas import tpu as pltpu
from jax.sharding import PartitionSpec as P

FIELDS = 4
GAIN = 0.2
MESH = pl.DeviceIdType.MESH
f32, bf16 = jnp.float32, jnp.bfloat16


def split_cat(w):
    hi = w.astype(bf16)
    lo = (w - hi.astype(f32)).astype(bf16)
    return jnp.concatenate(
        [jnp.concatenate([hi, hi], axis=1), jnp.concatenate([lo, lo], axis=1)], axis=0
    )


def col(cat, field):
    n = field.shape[0]
    hi = field.astype(bf16)
    lo = (field - hi.astype(f32)).astype(bf16)
    r = jnp.dot(cat, jnp.concatenate([hi, lo], axis=0), preferred_element_type=f32)
    return r[:n] + r[n:]


def rounded(v):
    return v.astype(bf16).astype(f32)


def lane_shifts(v, lo, hi):
    n = v.shape[1]
    lane = lax.broadcasted_iota(jnp.int32, v.shape, 1)
    down = jnp.where(lane == 0, lo, pltpu.roll(v, 1, 1))
    up = jnp.where(lane == n - 1, hi, pltpu.roll(v, n - 1, 1))
    return down + up


def row_iota():
    return lax.broadcasted_iota(jnp.int32, (8, 128), 0)


def kernel(
    nx, ny, air_x, sea_x,
    av, sv, asc, ssc, aw, sw, wa, wo, mask, fidx, fcnt, ftil, sidx, scnt, stil,
    aout, sout,
    av_s, sv_s, as_s, ss_s, aw_s, sw_s, wa_s, wo_s, mask_s, fidx_s, fcnt_s, ft_s, sidx_s, scnt_s, st_s,
    wcat, wcat_t, ocat, ocat_t, mf,
    at, s1, adj, au, so, ao,
    dx_f, dx_s, S_a, S_o, L_f, L_s, F, G, A_f, A_s, Cf, Cs, R_f, R_s,
    xl_a, xr_a, xl_o, xr_o, e_lo, e_hi, h_lo, h_hi,
    xl2_a, xr2_a, xl2_o, xr2_o, e2_lo, e2_hi, h2_lo, h2_hi,
    in_sem, out_sem, send_sem, recv_sem,
):
    gx, gy = lax.axis_index("gx"), lax.axis_index("gy")
    right, left = lax.rem(gx + 1, nx), lax.rem(gx + nx - 1, nx)
    above, below = lax.rem(gy + 1, ny), lax.rem(gy + ny - 1, ny)
    to_right, to_left = (right, gy), (left, gy)
    to_above, to_below = (gx, above), (gx, below)

    def load_columns(src, dst, sem, count):
        for x in range(count):
            pltpu.make_async_copy(src.at[:, x, :], dst.at[x], in_sem.at[sem]).start()

    def loaded(dst, sem):
        pltpu.make_async_copy(dst, dst, in_sem.at[sem]).wait()

    def load(src, dst, sem):
        pltpu.make_async_copy(src, dst, in_sem.at[sem]).start()

    barrier = pltpu.get_barrier_semaphore()
    for device in (to_right, to_left, to_above, to_below):
        pl.semaphore_signal(barrier, inc=1, device_id=device, device_id_type=MESH)

    load(mask, mask_s, 0)
    load_columns(sv, sv_s, 1, sea_x)
    load_columns(av, av_s, 2, air_x)
    load(wa, wa_s, 3)
    load(wo, wo_s, 4)
    load(fidx.at[0], fidx_s, 5)
    load(fcnt, fcnt_s, 6)
    load(sidx.at[0], sidx_s, 7)
    load(scnt, scnt_s, 8)
    load_columns(asc, as_s, 9, air_x)
    load(ftil.at[0], ft_s, 10)
    load(stil.at[0], st_s, 11)
    load_columns(ssc, ss_s, 12, sea_x)
    load_columns(sw, sw_s, 13, sea_x)
    load_columns(aw, aw_s, 14, air_x)

    pl.semaphore_wait(barrier, 4)

    def remote(src, dst, k, device):
        return pltpu.make_async_remote_copy(
            src_ref=src, dst_ref=dst, send_sem=send_sem.at[k], recv_sem=recv_sem.at[k],
            device_id=device, device_id_type=MESH,
        )

    halo_xr = remote(av.at[:, air_x - 1, :], xl_a, 0, to_right)
    halo_xl = remote(av.at[:, 0, :], xr_a, 1, to_left)
    halo_xr.start()
    halo_xl.start()

    loaded(mask_s, 0)
    mf[...] = mask_s[...].astype(f32)
    loaded(sv_s, 1)

    lane64 = lax.broadcasted_iota(jnp.int32, (64, 128), 1)
    zero64 = jnp.zeros((64, 128), f32)

    def sea_zero(x, acc):
        lo, hi = acc
        z = mf[x:x + 1, :] * sv_s[x]
        sv_s[x] = z
        here = lane64 == x + 2 * air_x
        lo = jnp.where(here, z[:, 0:1], lo)
        hi = jnp.where(here, z[:, -1:], hi)
        return lo, hi

    edges = (zero64, zero64)
    for x in range(sea_x):
        edges = sea_zero(x, edges)
    halo_or = remote(sv_s.at[sea_x - 1], xl_o, 2, to_right)
    halo_ol = remote(sv_s.at[0], xr_o, 3, to_left)
    halo_or.start()
    halo_ol.start()

    loaded(av_s, 2)

    def pack_air(field, x, acc):
        lo, hi = acc
        for part in range(2):
            v = field[64 * part:64 * part + 64]
            here = lane64 == x + part * air_x
            lo = jnp.where(here, v[:, 0:1], lo)
            hi = jnp.where(here, v[:, -1:], hi)
        return lo, hi

    for x in range(air_x):
        edges = pack_air(av_s[x], x, edges)
    e_lo[...], e_hi[...] = edges
    halo_yu = remote(e_hi, h_lo, 4, to_above)
    halo_yd = remote(e_lo, h_hi, 5, to_below)
    halo_yu.start()
    halo_yd.start()

    loaded(wa_s, 3)
    loaded(wo_s, 4)
    wcat[...] = split_cat(wa_s[...])
    wcat_t[...] = split_cat(wa_s[...].T)
    ocat[...] = split_cat(wo_s[...])
    ocat_t[...] = split_cat(wo_s[...].T)

    row_blocks = 32 * nx

    def places(idx_s, cnt_s, dx):
        own = gx * 32 + lax.broadcasted_iota(jnp.int32, (4, 32), 1)
        rel = idx_s[...] - own
        d = jnp.where(rel == 0, 0.0, jnp.where((rel == 1) | (rel == 1 - row_blocks), 1.0, -1.0))
        block = lax.broadcasted_iota(jnp.int32, (128, 32), 0) // 4
        pick = jnp.where(block == lax.broadcasted_iota(jnp.int32, (128, 32), 1), 1.0, 0.0)
        count = cnt_s[...].astype(f32)
        for k in range(4):
            dk = jnp.where(count > k, d[k:k + 1, :], 2.0)
            dx[k] = jnp.broadcast_to(jnp.sum(pick * dk, axis=1, keepdims=True), (128, 128))

    loaded(fidx_s, 5)
    loaded(fcnt_s, 6)
    places(fidx_s, fcnt_s, dx_f)
    loaded(sidx_s, 7)
    loaded(scnt_s, 8)
    places(sidx_s, scnt_s, dx_s)

    halo_xl.wait()
    halo_xr.wait()
    halo_ol.wait()
    halo_or.wait()
    halo_yu.wait()
    halo_yd.wait()

    def zero_outside(h):
        lo = jnp.where(gy == 0, 0.0, h[0][...])
        hi = jnp.where(gy == ny - 1, 0.0, h[1][...])
        h[0][...] = lo
        h[1][...] = hi

    zero_outside((h_lo, h_hi))

    def pick_lane(packed, lane):
        return packed[:, lane:lane + 1]

    def air_ends(hl, hh, x):
        lo = jnp.concatenate([pick_lane(hl[...], x), pick_lane(hl[...], x + air_x)], axis=0)
        hi = jnp.concatenate([pick_lane(hh[...], x), pick_lane(hh[...], x + air_x)], axis=0)
        return lo, hi

    def sea_ends(hl, hh, x):
        return pick_lane(hl[...], x + 2 * air_x), pick_lane(hh[...], x + 2 * air_x)

    loaded(as_s, 9)
    half = row_iota() < 4

    def air_first(x, west, east):
        v = av_s[x]
        lo, hi = air_ends(h_lo, h_hi, x)
        one = GAIN * (v + west + east + lane_shifts(v, lo, hi))
        two = col(wcat[...], as_s[x] * one)
        at[x] = two
        low = rounded(two[120:128])
        slab = jnp.where(half, pltpu.roll(low[:, 0:128], 4, 0), low[:, 128:256])
        S_a[pl.ds(8 + 8 * x, 8), :] = slab

    air_first(0, xl_a[...], av_s[1])
    air_first(air_x - 1, av_s[air_x - 2], xr_a[...])

    def send_rims(src_hi, src_lo, dst_hi, dst_lo, k):
        up = remote(src_hi.at[128:136], dst_hi.at[0:8], k, to_right)
        down = remote(src_lo.at[8:16], dst_lo.at[136:144], k + 1, to_left)
        up.start()
        down.start()
        return up, down

    rim_a = send_rims(S_a, S_a, S_a, S_a, 6)

    def sea_first(x, west, east):
        v = sv_s[x]
        m = mf[x:x + 1, :]
        lo, hi = sea_ends(h_lo, h_hi, x)
        one = v + (GAIN * m) * (west + east + lane_shifts(v, lo, hi) - 4.0 * v)
        s1[x] = one
        top = rounded(one[0:8])
        for q in range(2):
            a = top[:, 256 * q:256 * q + 128]
            b = top[:, 256 * q + 128:256 * q + 256]
            slab = jnp.where(half, a, pltpu.roll(b, 4, 0))
            S_o[pl.ds(8 + 16 * x + 8 * q, 8), :] = slab

    sea_first(0, xl_o[...], sv_s[1])
    sea_first(sea_x - 1, sv_s[sea_x - 2], xr_o[...])
    rim_o = send_rims(S_o, S_o, S_o, S_o, 8)

    for x in range(1, sea_x - 1):
        sea_first(x, sv_s[x - 1], sv_s[x + 1])

    for x in range(1, air_x - 1):
        air_first(x, av_s[x - 1], av_s[x + 1])

    def gather_rows(S, dx, L, r0, r1):
        s_m, s_0, s_p = S[4 + r0:4 + r1], S[8 + r0:8 + r1], S[12 + r0:12 + r1]
        for k in range(4):
            d = dx[k, r0:r1]
            L[r0:r1, 128 * k:128 * k + 128] = jnp.where(
                d == 0.0, s_0, jnp.where(d == -1.0, s_m, jnp.where(d == 1.0, s_p, 0.0))
            )

    def pair_tiles(T, p):
        return jnp.concatenate(
            [jnp.concatenate([T[2 * p + a, k] for k in range(4)], axis=1) for a in range(2)], axis=0
        )

    def pair_rows(p):
        return pl.ds(8 * p, 8)

    def forward_pair(L, T, out, p):
        r = lax.dot_general(
            L[pair_rows(p), :].astype(bf16), pair_tiles(T, p), (((1,), (1,)), ((), ())),
            preferred_element_type=f32,
        )
        out[pair_rows(p), :] = jnp.where(half, r[:, 0:128], r[:, 128:256])

    def back_pair(A, T, dx, C, p):
        a = A[pair_rows(p), :]
        lhs = jnp.concatenate([jnp.where(half, a, 0.0), jnp.where(half, 0.0, a)], axis=1)
        r = jnp.dot(lhs.astype(bf16), pair_tiles(T, p), preferred_element_type=f32)
        sums = [jnp.zeros((8, 128), f32) for _ in range(3)]
        for k in range(4):
            d = dx[k, pair_rows(p), :]
            c = r[:, 128 * k:128 * k + 128]
            for n in range(3):
                sums[n] = sums[n] + jnp.where(d == n - 1.0, c, 0.0)
        for n in range(3):
            C[n, pl.ds(8 + 8 * p, 8), :] = sums[n]

    gather_rows(S_a, dx_f, L_f, 8, 120)
    gather_rows(S_o, dx_s, L_s, 8, 120)
    loaded(ft_s, 10)
    loaded(st_s, 11)

    for p in range(1, 15):
        forward_pair(L_f, ft_s, F, p)
        forward_pair(L_s, st_s, G, p)

    for c in rim_a + rim_o:
        c.wait()
    for r0 in (0, 120):
        gather_rows(S_a, dx_f, L_f, r0, r0 + 8)
        gather_rows(S_o, dx_s, L_s, r0, r0 + 8)
    for p in (0, 15):
        forward_pair(L_f, ft_s, F, p)
        forward_pair(L_s, st_s, G, p)

    loaded(ss_s, 12)
    loaded(sw_s, 13)

    def sea_top(slabs):
        parts = []
        for slab in slabs:
            parts.append(jnp.where(half, slab, 0.0))
            parts.append(jnp.where(half, pltpu.roll(slab, 4, 0), 0.0))
        return jnp.concatenate(parts, axis=1)

    def sea_slabs(ref, x):
        return [ref[pl.ds(16 * x + 8 * q, 8), :] for q in range(2)]

    def sea_columns(x):
        m = mf[x:x + 1, :]
        one = s1[x]
        two = jnp.concatenate([one[0:8] + m * sea_top(sea_slabs(F, x)), one[8:]], axis=0)
        three = col(ocat[...], ss_s[x] * two)
        back = ss_s[x] * col(ocat_t[...], m * (sw_s[x] * three))
        adj[x] = back
        top = rounded(m * back[0:8])
        for q in range(2):
            a = top[:, 256 * q:256 * q + 128]
            b = top[:, 256 * q + 128:256 * q + 256]
            A_f[pl.ds(16 * x + 8 * q, 8), :] = jnp.where(half, a, pltpu.roll(b, 4, 0))

    sea_columns(0)
    sea_columns(sea_x - 1)
    for p in (0, 15):
        back_pair(A_f, ft_s, dx_f, Cf, p)
    rim_f = send_rims(Cf.at[2], Cf.at[0], Cf.at[2], Cf.at[0], 10)

    loaded(aw_s, 14)

    def air_low(ref, x):
        slab = ref[pl.ds(8 * x, 8), :]
        return jnp.concatenate(
            [jnp.where(half, 0.0, pltpu.roll(slab, 4, 0)), jnp.where(half, 0.0, slab)], axis=1
        )

    def air_forcing(x):
        two = at[x]
        three = jnp.concatenate([two[0:120], two[120:128] + air_low(G, x)], axis=0)
        forcing = aw_s[x] * three
        at[x] = forcing
        low = rounded(forcing[120:128])
        A_s[pl.ds(8 * x, 8), :] = jnp.where(
            half, pltpu.roll(low[:, 0:128], 4, 0), low[:, 128:256]
        )

    air_forcing(0)
    air_forcing(air_x - 1)
    for p in (0, 15):
        back_pair(A_s, st_s, dx_s, Cs, p)
    rim_s = send_rims(Cs.at[2], Cs.at[0], Cs.at[2], Cs.at[0], 12)

    for x in range(1, sea_x - 1):
        sea_columns(x)

    for x in range(1, air_x - 1):
        air_forcing(x)

    for p in range(1, 15):
        back_pair(A_f, ft_s, dx_f, Cf, p)
        back_pair(A_s, st_s, dx_s, Cs, p)

    for c in rim_f + rim_s:
        c.wait()
    R_f[...] = Cf[1, 8:136] + Cf[0, 12:140] + Cf[2, 4:132]
    R_s[...] = Cs[1, 8:136] + Cs[0, 12:140] + Cs[2, 4:132]

    def sea_upper(x):
        back = adj[x]
        up = jnp.concatenate([back[0:8] + sea_top(sea_slabs(R_s, x)), back[8:]], axis=0)
        z = mf[x:x + 1, :] * up
        adj[x] = z
        return z

    def air_upper(x):
        low = at[x]
        low = jnp.concatenate([low[0:120], low[120:128] + air_low(R_f, x)], axis=0)
        up = as_s[x] * col(wcat_t[...], low)
        au[x] = up
        return up

    def pack_sea(z, x, acc):
        lo, hi = acc
        here = lane64 == x + 2 * air_x
        return jnp.where(here, z[:, 0:1], lo), jnp.where(here, z[:, -1:], hi)

    edges = (zero64, zero64)
    for x in (0, sea_x - 1):
        edges = pack_sea(sea_upper(x), x, edges)
    for x in (0, air_x - 1):
        edges = pack_air(air_upper(x), x, edges)
    last = [
        remote(au.at[air_x - 1], xl2_a, 14, to_right),
        remote(au.at[0], xr2_a, 15, to_left),
        remote(adj.at[sea_x - 1], xl2_o, 16, to_right),
        remote(adj.at[0], xr2_o, 17, to_left),
    ]
    for c in last:
        c.start()
    for x in range(1, sea_x - 1):
        edges = pack_sea(sea_upper(x), x, edges)
    for x in range(1, air_x - 1):
        edges = pack_air(air_upper(x), x, edges)
    e2_lo[...], e2_hi[...] = edges
    last += [remote(e2_hi, h2_lo, 18, to_above), remote(e2_lo, h2_hi, 19, to_below)]
    for c in last[4:]:
        c.start()
    for c in last:
        c.wait()
    zero_outside((h2_lo, h2_hi))

    def sea_last(x, west, east):
        z = adj[x]
        lo, hi = sea_ends(h2_lo, h2_hi, x)
        so[x] = z + (GAIN * mf[x:x + 1, :]) * (west + east + lane_shifts(z, lo, hi) - 4.0 * z)

    def air_last(x, west, east):
        v = au[x]
        lo, hi = air_ends(h2_lo, h2_hi, x)
        ao[x] = GAIN * (v + west + east + lane_shifts(v, lo, hi))

    sea_last(0, xl2_o[...], adj[1])
    sea_last(sea_x - 1, adj[sea_x - 2], xr2_o[...])

    for x in range(1, sea_x - 1):
        sea_last(x, adj[x - 1], adj[x + 1])

    for x in range(sea_x):
        pltpu.make_async_copy(so.at[x], sout.at[:, x, :], out_sem.at[0]).start()

    air_last(0, xl2_a[...], au[1])
    air_last(air_x - 1, au[air_x - 2], xr2_a[...])

    for x in range(1, air_x - 1):
        air_last(x, au[x - 1], au[x + 1])

    for x in range(air_x):
        pltpu.make_async_copy(ao.at[x], aout.at[:, x, :], out_sem.at[1]).start()
    pltpu.make_async_copy(so, so, out_sem.at[0]).wait()
    pltpu.make_async_copy(ao, ao, out_sem.at[1]).wait()


def shards(*args, nx, ny):
    av, sv = args[0], args[1]
    args = [a.transpose(0, 2, 1) if n in (9, 12) else a for n, a in enumerate(args)]
    levels, air_x, air_y = av.shape
    sea_levels, sea_x, sea_y = sv.shape
    V = pltpu.VMEM
    air = V((air_x, levels, air_y), f32)
    sea = V((sea_x, sea_levels, sea_y), f32)
    blk = V((128, 128), f32)
    ext = V((144, 128), f32)
    rowa, rowo, pack = V((levels, air_y), f32), V((sea_levels, sea_y), f32), V((64, 128), f32)
    tiles = V((32, 4, 128, 128), bf16)
    idx, cnt = V((4, 32), jnp.int32), V((1, 32), jnp.int32)
    wcat = V((2 * levels, 2 * levels), bf16)
    ocat = V((2 * sea_levels, 2 * sea_levels), bf16)
    dx = V((4, 128, 128), f32)
    cterm = V((3, 144, 128), f32)
    dma = pltpu.SemaphoreType.DMA
    scratch = [
        air, sea, air, sea, air, sea, V((levels, levels), f32), V((sea_levels, sea_levels), f32),
        V((sea_x, sea_y), jnp.int32), idx, cnt, tiles, idx, cnt, tiles,
        wcat, wcat, ocat, ocat, V((sea_x, sea_y), f32),
        air, sea, sea, air, sea, air,
        dx, dx, ext, ext, V((128, 512), f32), V((128, 512), f32), blk, blk, blk, blk, cterm, cterm, blk, blk,
        rowa, rowa, rowo, rowo, pack, pack, pack, pack,
        rowa, rowa, rowo, rowo, pack, pack, pack, pack,
        dma((15,)), dma((2,)), dma((20,)), dma((20,)),
    ]
    anywhere = pl.BlockSpec(memory_space=pl.ANY)
    return pl.pallas_call(
        functools.partial(kernel, nx, ny, air_x, sea_x),
        out_shape=(jax.ShapeDtypeStruct(av.shape, f32), jax.ShapeDtypeStruct(sv.shape, f32)),
        in_specs=[anywhere] * 15,
        out_specs=(anywhere, anywhere),
        scratch_shapes=scratch,
        compiler_params=pltpu.CompilerParams(
            collective_id=0, has_side_effects=True, vmem_limit_bytes=56 * 1024 * 1024
        ),
        cost_estimate=pl.CostEstimate(flops=4_000_000_000, bytes_accessed=21_000_000, transcendentals=0),
    )(*args)


def solution(mesh):
    grid = P(None, "gx", "gy")
    index, count, tiles = P("gy", "gx", None), P("gy", "gx"), P("gy", "gx", None, None, None)
    return jax.shard_map(
        functools.partial(shards, nx=mesh.shape["gx"], ny=mesh.shape["gy"]),
        mesh=mesh,
        in_specs=(grid,) * 6 + (P(), P(), P("gx", "gy"), index, count, tiles, index, count, tiles),
        out_specs=(grid, grid),
        check_vma=False,
    )
```

```python
import functools

import jax
import jax.numpy as jnp
from jax import lax
from jax.experimental import pallas as pl
from jax.experimental.pallas import tpu as pltpu
from jax.sharding import PartitionSpec as P

GAIN = 0.2
MESH = pl.DeviceIdType.MESH
f32, bf16 = jnp.float32, jnp.bfloat16


def split_cat(w):
    hi = w.astype(bf16)
    lo = (w - hi.astype(f32)).astype(bf16)
    return jnp.concatenate(
        [jnp.concatenate([hi, hi], axis=1), jnp.concatenate([lo, lo], axis=1)], axis=0
    )


def col(cat, field):
    n = field.shape[0]
    hi = field.astype(bf16)
    lo = (field - hi.astype(f32)).astype(bf16)
    r = jnp.dot(cat, jnp.concatenate([hi, lo], axis=0), preferred_element_type=f32)
    return r[:n] + r[n:]


def rounded(v):
    return v.astype(bf16).astype(f32)


def lane_of(v):
    return lax.broadcasted_iota(jnp.int32, v.shape, 1)


def lane_shifts(v):
    n = v.shape[1]
    lane = lane_of(v)
    down = jnp.where(lane == 0, 0.0, pltpu.roll(v, 1, 1))
    up = jnp.where(lane == n - 1, 0.0, pltpu.roll(v, n - 1, 1))
    return down + up


def with_ends(v, lo, hi):
    head, tail = v[:, :128], v[:, -128:]
    lane = lane_of(head)
    head = jnp.where(lane == 0, head + lo, head)
    tail = jnp.where(lane == 127, tail + hi, tail)
    return jnp.concatenate([head, v[:, 128:-128], tail], axis=1) if v.shape[1] > 256 else jnp.concatenate(
        [head, tail], axis=1
    )


def put_ends(packed, field, lo, hi):
    lane = lane_of(packed)
    packed = jnp.where(lane == lo, field[:, 0:1], packed)
    return jnp.where(lane == hi, field[:, -1:], packed)


def kernel(
    nx, ny, air_x, sea_x,
    av, sv, asc, ssc, aw, sw, wa, wo, mask, fidx, fcnt, ftil, sidx, scnt, stil,
    ao, so,
    av_s, sv_s, as_s, ss_s, aw_s, sw_s, wa_s, wo_s, mask_s, fidx_s, fcnt_s, ft_s, sidx_s, scnt_s, st_s,
    wcat, wcat_t, ocat, ocat_t, mf,
    at, s1, adj, au,
    dx_f, dx_s, S_a, S_o, L_f, L_s, F, G, A_f, A_s, Cf, Cs, R_f, R_s,
    xl_a, xr_a, xl_o, xr_o, mine, from_lo, from_hi, halo_a, halo_o, as_p, fix, af_p,
    xl2_a, xr2_a, xl2_o, xr2_o, mine2, from_lo2, from_hi2, halo2_a, halo2_o,
    in_sem, send_sem, recv_sem,
):
    gx, gy = lax.axis_index("gx"), lax.axis_index("gy")
    right, left = lax.rem(gx + 1, nx), lax.rem(gx + nx - 1, nx)
    above, below = lax.rem(gy + 1, ny), lax.rem(gy + ny - 1, ny)
    to_right, to_left = (right, gy), (left, gy)
    to_above, to_below = (gx, above), (gx, below)
    last_a, last_o = air_x - 1, sea_x - 1

    def load_columns(src, dst, sem, count):
        for x in range(count):
            pltpu.make_async_copy(src.at[:, x, :], dst.at[x], in_sem.at[sem]).start()

    def loaded(dst, sem):
        pltpu.make_async_copy(dst, dst, in_sem.at[sem]).wait()

    def load(src, dst, sem):
        pltpu.make_async_copy(src, dst, in_sem.at[sem]).start()

    barrier = pltpu.get_barrier_semaphore()
    for device in (to_right, to_left, to_above, to_below):
        pl.semaphore_signal(barrier, inc=1, device_id=device, device_id_type=MESH)

    load(mask, mask_s, 0)
    load_columns(sv, sv_s, 1, sea_x)
    load_columns(av, av_s, 2, air_x)
    load(wa, wa_s, 3)
    load(wo, wo_s, 4)
    load(fidx.at[0], fidx_s, 5)
    load(fcnt, fcnt_s, 6)
    load(sidx.at[0], sidx_s, 7)
    load(scnt, scnt_s, 8)
    load_columns(asc, as_s, 9, air_x)
    load(ftil.at[0], ft_s, 10)
    load(stil.at[0], st_s, 11)
    load_columns(ssc, ss_s, 12, sea_x)
    load_columns(sw, sw_s, 13, sea_x)
    load_columns(aw, aw_s, 14, air_x)

    def remote(src, dst, k, device):
        return pltpu.make_async_remote_copy(
            src_ref=src, dst_ref=dst, send_sem=send_sem.at[k], recv_sem=recv_sem.at[k],
            device_id=device, device_id_type=MESH,
        )

    def start(*copies):
        for c in copies:
            c.start()
        return copies

    def wait(copies):
        for c in copies:
            c.wait()

    half = lax.broadcasted_iota(jnp.int32, (8, 128), 0) < 4

    def message(air_p, sea_p):
        lane = lane_of(sea_p)
        low = jnp.where(lane < 2 * air_x, air_p[:64], pltpu.roll(air_p[64:], 2 * air_x, 1))
        return jnp.where(lane < 4 * air_x, low, pltpu.roll(sea_p, 4 * air_x, 1))

    def open_messages(lo_ref, hi_ref, air_ref, sea_ref):
        lo = jnp.where(gy == 0, 0.0, lo_ref[...])
        hi = jnp.where(gy == ny - 1, 0.0, hi_ref[...])
        lane = lane_of(lo)
        air = jnp.where(
            lax.rem(lane, 2 * air_x) < air_x, pltpu.roll(lo, 128 - air_x, 1), pltpu.roll(hi, air_x, 1)
        )
        air_ref[...] = jnp.concatenate([air, pltpu.roll(air, 128 - 2 * air_x, 1)], axis=0)
        lo = pltpu.roll(lo, 128 - 4 * air_x - sea_x, 1)
        hi = pltpu.roll(hi, 128 - 4 * air_x + sea_x, 1)
        sea_ref[...] = jnp.where(lane < sea_x, lo, hi)

    def packed_air(ref):
        p = jnp.zeros((128, 128), f32)
        for x in range(air_x):
            p = put_ends(p, ref[x], x, air_x + x)
        return p

    def packed_sea(ref):
        p = jnp.zeros((64, 128), f32)
        for x in range(sea_x):
            p = put_ends(p, ref[x], x, sea_x + x)
        return p

    def phase_mask():
        loaded_mask = mask_s[...].astype(f32)
        mf[...] = loaded_mask
        for x in range(sea_x):
            sv_s[x] = loaded_mask[x:x + 1, :] * sv_s[x]

    def phase_pack():
        mine[...] = message(packed_air(av_s), packed_sea(sv_s))

    def phase_matrices():
        wcat[...] = split_cat(wa_s[...])
        wcat_t[...] = split_cat(wa_s[...].T)
        ocat[...] = split_cat(wo_s[...])
        ocat_t[...] = split_cat(wo_s[...].T)

    row_blocks = 32 * nx

    def places(idx_s, cnt_s, dx):
        own = gx * 32 + lax.broadcasted_iota(jnp.int32, (4, 32), 1)
        rel = idx_s[...] - own
        d = jnp.where(rel == 0, 0.0, jnp.where((rel == 1) | (rel == 1 - row_blocks), 1.0, -1.0))
        block = lax.broadcasted_iota(jnp.int32, (128, 32), 0) // 4
        pick = jnp.where(block == lax.broadcasted_iota(jnp.int32, (128, 32), 1), 1.0, 0.0)
        count = cnt_s[...].astype(f32)
        for k in range(4):
            dk = jnp.where(count > k, d[k:k + 1, :], 2.0)
            dx[k] = jnp.broadcast_to(jnp.sum(pick * dk, axis=1, keepdims=True), (128, 128))

    def phase_places():
        places(fidx_s, fcnt_s, dx_f)
        places(sidx_s, scnt_s, dx_s)

    def air_first(x, west, east):
        v = av_s[x]
        at[x] = col(wcat[...], as_s[x] * (GAIN * (v + west + east + lane_shifts(v))))

    def sea_first(x, west, east):
        v = sv_s[x]
        s1[x] = v + (GAIN * mf[x:x + 1, :]) * (west + east + lane_shifts(v) - 4.0 * v)

    def phase_air_first():
        for x in range(1, last_a):
            air_first(x, av_s[x - 1], av_s[x + 1])

    def phase_sea_first():
        for x in range(1, last_o):
            sea_first(x, sv_s[x - 1], sv_s[x + 1])

    def phase_as_pack():
        as_p[...] = packed_air(as_s)

    def phase_air_outer():
        air_first(0, xl_a[...], av_s[1])
        air_first(last_a, av_s[last_a - 1], xr_a[...])

    def phase_fix():
        fix[...] = col(wcat[...], as_p[...] * (GAIN * halo_a[...]))

    def air_ends(ref, x, rows=slice(None)):
        return ref[rows, x:x + 1], ref[rows, air_x + x:air_x + x + 1]

    def sea_ends(ref, x, rows=slice(None)):
        return ref[rows, x:x + 1], ref[rows, sea_x + x:sea_x + x + 1]

    def phase_air_surface():
        for x in range(air_x):
            low = rounded(with_ends(at[x, 120:128, :], *air_ends(fix, x, slice(120, 128))))
            S_a[8 + 8 * x:16 + 8 * x, :] = jnp.where(half, pltpu.roll(low[:, 0:128], 4, 0), low[:, 128:256])

    def sea_finish(x, v, rows):
        lo, hi = sea_ends(halo_o, x, rows)
        return with_ends(v, (GAIN * mf[x:x + 1, 0:1]) * lo, (GAIN * mf[x:x + 1, -1:]) * hi)

    def sea_outer(rows):
        for x, west, east in ((0, xl_o, sv_s.at[1]), (last_o, sv_s.at[last_o - 1], xr_o)):
            v = sv_s[x, rows, :]
            s1[x, rows, :] = v + (GAIN * mf[x:x + 1, :]) * (
                west[rows, :] + east[rows, :] + lane_shifts(v) - 4.0 * v
            )

    def to_slabs(top):
        out = []
        for q in range(2):
            a, b = top[:, 256 * q:256 * q + 128], top[:, 256 * q + 128:256 * q + 256]
            out.append(jnp.where(half, a, pltpu.roll(b, 4, 0)))
        return jnp.concatenate(out, axis=0)

    def phase_sea_surface():
        sea_outer(slice(0, 8))
        for x in range(sea_x):
            top = sea_finish(x, s1[x, 0:8, :], slice(0, 8))
            S_o[8 + 16 * x:24 + 16 * x, :] = to_slabs(rounded(top))

    def phase_sea_outer():
        sea_outer(slice(8, 64))

    def send_rims(src_hi, src_lo, k):
        return start(
            remote(src_hi.at[128:136], src_hi.at[0:8], k, to_right),
            remote(src_lo.at[8:16], src_lo.at[136:144], k + 1, to_left),
        )

    def gather_rows(S, dx, L, r0, r1):
        s_m, s_0, s_p = S[4 + r0:4 + r1], S[8 + r0:8 + r1], S[12 + r0:12 + r1]
        for k in range(4):
            d = dx[k, r0:r1]
            L[r0:r1, 128 * k:128 * k + 128] = jnp.where(
                d == 0.0, s_0, jnp.where(d == -1.0, s_m, jnp.where(d == 1.0, s_p, 0.0))
            )

    def pair_tiles(T, p):
        return jnp.concatenate(
            [jnp.concatenate([T[2 * p + a, k] for k in range(4)], axis=1) for a in range(2)], axis=0
        )

    def forward_pair(L, T, out, p):
        r = lax.dot_general(
            L[8 * p:8 * p + 8, :].astype(bf16), pair_tiles(T, p), (((1,), (1,)), ((), ())),
            preferred_element_type=f32,
        )
        out[8 * p:8 * p + 8, :] = jnp.where(half, r[:, 0:128], r[:, 128:256])

    def back_pair(A, T, dx, C, p):
        a = A[8 * p:8 * p + 8, :]
        lhs = jnp.concatenate([jnp.where(half, a, 0.0), jnp.where(half, 0.0, a)], axis=1)
        r = jnp.dot(lhs.astype(bf16), pair_tiles(T, p), preferred_element_type=f32)
        sums = [jnp.zeros((8, 128), f32) for _ in range(3)]
        for k in range(4):
            d = dx[k, 8 * p:8 * p + 8, :]
            c = r[:, 128 * k:128 * k + 128]
            for n in range(3):
                sums[n] = sums[n] + jnp.where(d == n - 1.0, c, 0.0)
        for n in range(3):
            C[n, 8 + 8 * p:16 + 8 * p, :] = sums[n]

    def phase_forward_skin():
        gather_rows(S_o, dx_s, L_s, 8, 120)
        for p in range(1, 15):
            forward_pair(L_s, st_s, G, p)

    def phase_forward_flux():
        gather_rows(S_a, dx_f, L_f, 8, 120)
        for p in range(1, 15):
            forward_pair(L_f, ft_s, F, p)

    def phase_forward_rims():
        for r0 in (0, 120):
            gather_rows(S_a, dx_f, L_f, r0, r0 + 8)
            gather_rows(S_o, dx_s, L_s, r0, r0 + 8)
        for p in (0, 15):
            forward_pair(L_f, ft_s, F, p)
            forward_pair(L_s, st_s, G, p)

    def sea_top(ref, x):
        parts = []
        for q in range(2):
            slab = ref[16 * x + 8 * q:16 * x + 8 * q + 8, :]
            parts.append(jnp.where(half, slab, 0.0))
            parts.append(jnp.where(half, pltpu.roll(slab, 4, 0), 0.0))
        return jnp.concatenate(parts, axis=1)

    def sea_columns(x):
        m = mf[x:x + 1, :]
        one = sea_finish(x, s1[x], slice(None))
        two = jnp.concatenate([one[0:8] + m * sea_top(F, x), one[8:]], axis=0)
        three = col(ocat[...], ss_s[x] * two)
        back = m * (ss_s[x] * col(ocat_t[...], m * (sw_s[x] * three)))
        adj[x] = back
        A_f[16 * x:16 * x + 16, :] = to_slabs(rounded(back[0:8]))

    def phase_sea_columns_outer():
        sea_columns(0)
        sea_columns(last_o)

    def phase_sea_columns():
        for x in range(1, last_o):
            sea_columns(x)

    def air_low(ref, x):
        slab = ref[8 * x:8 * x + 8, :]
        return jnp.concatenate(
            [jnp.where(half, 0.0, pltpu.roll(slab, 4, 0)), jnp.where(half, 0.0, slab)], axis=1
        )

    def air_forcing(x):
        two = with_ends(at[x], *air_ends(fix, x))
        three = jnp.concatenate([two[0:120], two[120:128] + air_low(G, x)], axis=0)
        forcing = aw_s[x] * three
        at[x] = forcing
        low = rounded(forcing[120:128])
        A_s[8 * x:8 * x + 8, :] = jnp.where(half, pltpu.roll(low[:, 0:128], 4, 0), low[:, 128:256])

    def phase_air_forcing_outer():
        air_forcing(0)
        air_forcing(last_a)

    def phase_air_forcing():
        for x in range(1, last_a):
            air_forcing(x)

    def phase_air_pack():
        af_p[...] = packed_air(at)

    def phase_back_flux_rims():
        for p in (0, 15):
            back_pair(A_f, ft_s, dx_f, Cf, p)

    def phase_back_skin_rims():
        for p in (0, 15):
            back_pair(A_s, st_s, dx_s, Cs, p)

    def phase_back_flux():
        for p in range(1, 15):
            back_pair(A_f, ft_s, dx_f, Cf, p)

    def phase_back_skin():
        for p in range(1, 15):
            back_pair(A_s, st_s, dx_s, Cs, p)

    def arrived(C, R, r0, r1):
        R[r0:r1, :] = C[1, r0 + 8:r1 + 8] + C[0, r0 + 12:r1 + 12] + C[2, r0 + 4:r1 + 4]

    def sea_upper(xs):
        for x in xs:
            adj[x, 0:8, :] = adj[x, 0:8, :] + mf[x:x + 1, :] * sea_top(R_s, x)

    def air_lower(xs):
        p = af_p[120:128, :]
        for x in xs:
            low = at[x, 120:128, :] + air_low(R_f, x)
            at[x, 120:128, :] = low
            p = put_ends(p, low, x, air_x + x)
        af_p[120:128, :] = p

    def phase_sea_upper():
        arrived(Cs, R_s, 16, 112)
        sea_upper(range(1, last_o))

    def phase_air_lower():
        arrived(Cf, R_f, 8, 120)
        air_lower(range(1, last_a))

    def phase_sea_upper_outer():
        arrived(Cs, R_s, 0, 16)
        arrived(Cs, R_s, 112, 128)
        sea_upper((0, last_o))

    def phase_air_lower_outer():
        arrived(Cf, R_f, 0, 8)
        arrived(Cf, R_f, 120, 128)
        air_lower((0, last_a))

    def phase_pack_last():
        air_p = as_p[...] * col(wcat_t[...], af_p[...])
        mine2[...] = message(air_p, packed_sea(adj))

    def air_upper(x):
        au[x] = as_s[x] * col(wcat_t[...], at[x])

    def phase_air_upper_outer():
        air_upper(0)
        air_upper(last_a)

    def phase_air_upper():
        for x in range(1, last_a):
            air_upper(x)

    def sea_last(x, west, east):
        z = adj[x]
        so[x] = z + (GAIN * mf[x:x + 1, :]) * (west + east + lane_shifts(z) - 4.0 * z)

    def air_last(x, west, east):
        v = au[x]
        ao[x] = GAIN * (v + west + east + lane_shifts(v))

    def phase_last():
        for x in range(1, last_o):
            sea_last(x, adj[x - 1], adj[x + 1])
        for x in range(1, last_a):
            air_last(x, au[x - 1], au[x + 1])

    def last_ends(sea_xs, air_xs):
        for x in sea_xs:
            lo, hi = sea_ends(halo2_o, x)
            so[x] = with_ends(so[x], (GAIN * mf[x:x + 1, 0:1]) * lo, (GAIN * mf[x:x + 1, -1:]) * hi)
        for x in air_xs:
            lo, hi = air_ends(halo2_a, x)
            ao[x] = with_ends(ao[x], GAIN * lo, GAIN * hi)

    def last_outer():
        sea_last(0, xl2_o[...], adj[1])
        sea_last(last_o, adj[last_o - 1], xr2_o[...])
        air_last(0, xl2_a[...], au[1])
        air_last(last_a, au[last_a - 1], xr2_a[...])
        last_ends((0, last_o), (0, last_a))

    pl.semaphore_wait(barrier, 4)
    halo_a1 = start(
        remote(av.at[:, last_a, :], xl_a, 0, to_right),
        remote(av.at[:, 0, :], xr_a, 1, to_left),
    )
    loaded(mask_s, 0)
    loaded(sv_s, 1)
    phase_mask()
    halo_o1 = start(
        remote(sv_s.at[last_o, 0:8], xl_o.at[0:8], 2, to_right),
        remote(sv_s.at[0, 0:8], xr_o.at[0:8], 3, to_left),
    )
    loaded(av_s, 2)
    phase_pack()
    halo_y1 = start(remote(mine, from_lo, 4, to_above), remote(mine, from_hi, 5, to_below))
    halo_o1_rest = start(
        remote(sv_s.at[last_o, 8:64], xl_o.at[8:64], 14, to_right),
        remote(sv_s.at[0, 8:64], xr_o.at[8:64], 15, to_left),
    )
    loaded(wa_s, 3)
    loaded(wo_s, 4)
    phase_matrices()
    loaded(fidx_s, 5)
    loaded(fcnt_s, 6)
    loaded(sidx_s, 7)
    loaded(scnt_s, 8)
    phase_places()
    phase_sea_first()
    loaded(as_s, 9)
    phase_air_first()
    phase_as_pack()

    wait(halo_y1)
    open_messages(from_lo, from_hi, halo_a, halo_o)
    phase_fix()
    wait(halo_o1)
    phase_sea_surface()
    rim_o = send_rims(S_o, S_o, 8)
    wait(halo_a1)
    phase_air_outer()
    phase_air_surface()
    rim_a = send_rims(S_a, S_a, 6)

    loaded(st_s, 11)
    phase_forward_skin()
    loaded(ft_s, 10)
    phase_forward_flux()
    loaded(ss_s, 12)
    loaded(sw_s, 13)
    phase_sea_columns()
    wait(rim_a)
    wait(rim_o)
    phase_forward_rims()
    wait(halo_o1_rest)
    phase_sea_outer()
    phase_sea_columns_outer()
    loaded(aw_s, 14)
    phase_air_forcing_outer()
    phase_back_flux_rims()
    phase_back_skin_rims()
    rim_f = send_rims(Cf.at[2], Cf.at[0], 10)
    rim_s = send_rims(Cs.at[2], Cs.at[0], 12)
    halo_o2_rest = start(
        remote(adj.at[last_o, 8:64], xl2_o.at[8:64], 16, to_right),
        remote(adj.at[0, 8:64], xr2_o.at[8:64], 17, to_left),
    )
    phase_air_forcing()
    phase_air_pack()
    phase_back_flux()
    phase_air_lower()
    phase_back_skin()
    phase_sea_upper()
    phase_air_upper()

    wait(rim_f)
    phase_air_lower_outer()
    phase_air_upper_outer()
    halo_a2 = start(remote(au.at[last_a], xl2_a, 18, to_right), remote(au.at[0], xr2_a, 19, to_left))
    wait(rim_s)
    phase_sea_upper_outer()
    halo_o2 = start(
        remote(adj.at[last_o, 0:8], xl2_o.at[0:8], 20, to_right),
        remote(adj.at[0, 0:8], xr2_o.at[0:8], 21, to_left),
    )
    phase_pack_last()
    halo_y2 = start(remote(mine2, from_lo2, 22, to_above), remote(mine2, from_hi2, 23, to_below))
    phase_last()
    wait(halo_y2)
    open_messages(from_lo2, from_hi2, halo2_a, halo2_o)
    last_ends(range(1, last_o), range(1, last_a))
    wait(halo_o2_rest)
    wait(halo_o2)
    wait(halo_a2)
    last_outer()


def deliver(a, o, aout, sout, sem):
    for x in range(a.shape[0]):
        pltpu.make_async_copy(a.at[x], aout.at[:, x, :], sem.at[0]).start()
    for x in range(o.shape[0]):
        pltpu.make_async_copy(o.at[x], sout.at[:, x, :], sem.at[1]).start()
    pltpu.make_async_copy(a, a, sem.at[0]).wait()
    pltpu.make_async_copy(o, o, sem.at[1]).wait()


def shards(*args, nx, ny):
    av, sv = args[0], args[1]
    args = [a.transpose(0, 2, 1) if n in (9, 12) else a for n, a in enumerate(args)]
    args = [pltpu.with_memory_space_constraint(a, pltpu.HBM) for a in args]
    levels, air_x, air_y = av.shape
    sea_levels, sea_x, sea_y = sv.shape
    V = pltpu.VMEM
    air = V((air_x, levels, air_y), f32)
    sea = V((sea_x, sea_levels, sea_y), f32)
    blk = V((128, 128), f32)
    ext = V((144, 128), f32)
    rowa, rowo, pack = V((levels, air_y), f32), V((sea_levels, sea_y), f32), V((64, 128), f32)
    tiles = V((32, 4, 128, 128), bf16)
    idx, cnt = V((4, 32), jnp.int32), V((1, 32), jnp.int32)
    wcat = V((2 * levels, 2 * levels), bf16)
    ocat = V((2 * sea_levels, 2 * sea_levels), bf16)
    dx = V((4, 128, 128), f32)
    cterm = V((3, 144, 128), f32)
    dma = pltpu.SemaphoreType.DMA
    scratch = [
        air, sea, air, sea, air, sea, V((levels, levels), f32), V((sea_levels, sea_levels), f32),
        V((sea_x, sea_y), jnp.int32), idx, cnt, tiles, idx, cnt, tiles,
        wcat, wcat, ocat, ocat, V((sea_x, sea_y), f32),
        air, sea, sea, air,
        dx, dx, ext, ext, V((128, 512), f32), V((128, 512), f32), blk, blk, blk, blk, cterm, cterm, blk, blk,
        rowa, rowa, rowo, rowo, pack, pack, pack, blk, pack, blk, blk, blk,
        rowa, rowa, rowo, rowo, pack, pack, pack, blk, pack,
        dma((15,)), dma((24,)), dma((24,)),
    ]
    anywhere = pl.BlockSpec(memory_space=pl.ANY)
    outs = (jax.ShapeDtypeStruct(av.shape, f32), jax.ShapeDtypeStruct(sv.shape, f32))
    held = pl.pallas_call(
        functools.partial(kernel, nx, ny, air_x, sea_x),
        out_shape=(air, sea),
        in_specs=[pl.BlockSpec(memory_space=pltpu.HBM)] * 15,
        out_specs=[pl.BlockSpec(memory_space=pltpu.VMEM)] * 2,
        scratch_shapes=scratch,
        compiler_params=pltpu.CompilerParams(
            collective_id=0, has_side_effects=True, vmem_limit_bytes=44 * 1024 * 1024
        ),
        cost_estimate=pl.CostEstimate(flops=4_000_000_000, bytes_accessed=21_000_000, transcendentals=0),
    )(*args)
    return pl.pallas_call(
        deliver,
        out_shape=outs,
        in_specs=[anywhere] * 2,
        out_specs=[pl.BlockSpec(memory_space=pltpu.HBM)] * 2,
        scratch_shapes=[dma((2,))],
        compiler_params=pltpu.CompilerParams(vmem_limit_bytes=1024 * 1024),
    )(*held)


def solution(mesh):
    grid = P(None, "gx", "gy")
    index, count, tiles = P("gy", "gx", None), P("gy", "gx"), P("gy", "gx", None, None, None)
    return jax.shard_map(
        functools.partial(shards, nx=mesh.shape["gx"], ny=mesh.shape["gy"]),
        mesh=mesh,
        in_specs=(grid,) * 6 + (P(), P(), P("gx", "gy"), index, count, tiles, index, count, tiles),
        out_specs=(grid, grid),
        check_vma=False,
    )
```

```python
import functools

import jax
import jax.numpy as jnp
from jax import lax
from jax.experimental import pallas as pl
from jax.experimental.pallas import tpu as pltpu
from jax.sharding import PartitionSpec as P

GAIN = 0.2
MESH = pl.DeviceIdType.MESH
f32, bf16 = jnp.float32, jnp.bfloat16


def split_cat(w):
    hi = w.astype(bf16)
    lo = (w - hi.astype(f32)).astype(bf16)
    return jnp.concatenate(
        [jnp.concatenate([hi, hi], axis=1), jnp.concatenate([lo, lo], axis=1)], axis=0
    )


def col(cat, field):
    n = field.shape[0]
    hi = field.astype(bf16)
    lo = (field - hi.astype(f32)).astype(bf16)
    r = jnp.dot(cat, jnp.concatenate([hi, lo], axis=0), preferred_element_type=f32)
    return r[:n] + r[n:]


def rounded(v):
    return v.astype(bf16).astype(f32)


def lane_of(v):
    return lax.broadcasted_iota(jnp.int32, v.shape, 1)


def lane_shifts(v):
    n = v.shape[1]
    lane = lane_of(v)
    down = jnp.where(lane == 0, 0.0, pltpu.roll(v, 1, 1))
    up = jnp.where(lane == n - 1, 0.0, pltpu.roll(v, n - 1, 1))
    return down + up


def with_ends(v, lo, hi):
    head, tail = v[:, :128], v[:, -128:]
    lane = lane_of(head)
    head = jnp.where(lane == 0, head + lo, head)
    tail = jnp.where(lane == 127, tail + hi, tail)
    return jnp.concatenate([head, v[:, 128:-128], tail], axis=1) if v.shape[1] > 256 else jnp.concatenate(
        [head, tail], axis=1
    )


def put_ends(packed, field, lo, hi):
    lane = lane_of(packed)
    packed = jnp.where(lane == lo, field[:, 0:1], packed)
    return jnp.where(lane == hi, field[:, -1:], packed)


def kernel(
    nx, ny, air_x, sea_x,
    av, sv, asc, ssc, aw, sw, wa, wo, mask, fidx, fcnt, ftil, sidx, scnt, stil,
    ao, so,
    av_s, sv_s, as_s, ss_s, aw_s, sw_s, wa_s, wo_s, mask_s, fidx_s, fcnt_s, ft_s, sidx_s, scnt_s, st_s,
    wcat, wcat_t, ocat, ocat_t, mf,
    at, s1, adj, au,
    dx_f, dx_s, S_a, S_o, L_f, L_s, F, G, A_f, A_s, Cf, Cs, R_f, R_s,
    xl_a, xr_a, xl_o, xr_o, mine, from_lo, from_hi, halo_a, halo_o, as_p, fix, af_p,
    xl2_a, xr2_a, xl2_o, xr2_o, mine2, from_lo2, from_hi2, halo2_a, halo2_o,
    own_l, own_r, top_l, top_r, as_l, as_r, m_l, m_r, df_lo, df_hi, ds_lo, ds_hi,
    in_sem, send_sem, recv_sem,
):
    gx, gy = lax.axis_index("gx"), lax.axis_index("gy")
    right, left = lax.rem(gx + 1, nx), lax.rem(gx + nx - 1, nx)
    above, below = lax.rem(gy + 1, ny), lax.rem(gy + ny - 1, ny)
    to_right, to_left = (right, gy), (left, gy)
    to_above, to_below = (gx, above), (gx, below)
    to_left_above, to_right_below = (left, above), (right, below)
    last_a, last_o = air_x - 1, sea_x - 1

    def load_columns(src, dst, sem, count):
        for x in range(count):
            pltpu.make_async_copy(src.at[:, x, :], dst.at[x], in_sem.at[sem]).start()

    def loaded(dst, sem):
        pltpu.make_async_copy(dst, dst, in_sem.at[sem]).wait()

    def load(src, dst, sem):
        pltpu.make_async_copy(src, dst, in_sem.at[sem]).start()

    barrier = pltpu.get_barrier_semaphore()
    for device in (to_right, to_left, to_above, to_below, to_left_above, to_right_below):
        pl.semaphore_signal(barrier, inc=1, device_id=device, device_id_type=MESH)

    load(mask, mask_s, 0)
    load_columns(sv, sv_s, 1, sea_x)
    load_columns(av, av_s, 2, air_x)
    load(wa, wa_s, 3)
    load(wo, wo_s, 4)
    load(fidx.at[0], fidx_s, 5)
    load(fcnt, fcnt_s, 6)
    load(sidx.at[0], sidx_s, 7)
    load(scnt, scnt_s, 8)
    load_columns(asc, as_s, 9, air_x)
    load(ftil.at[0], ft_s, 10)
    load(stil.at[0], st_s, 11)
    load_columns(ssc, ss_s, 12, sea_x)
    load_columns(sw, sw_s, 13, sea_x)
    load_columns(aw, aw_s, 14, air_x)

    def remote(src, dst, k, device):
        return pltpu.make_async_remote_copy(
            src_ref=src, dst_ref=dst, send_sem=send_sem.at[k], recv_sem=recv_sem.at[k],
            device_id=device, device_id_type=MESH,
        )

    def start(*copies):
        for c in copies:
            c.start()
        return copies

    def wait(copies):
        for c in copies:
            c.wait()

    half = lax.broadcasted_iota(jnp.int32, (8, 128), 0) < 4

    def message(air_p, sea_p):
        lane = lane_of(sea_p)
        low = jnp.where(lane < 2 * air_x, air_p[:64], pltpu.roll(air_p[64:], 2 * air_x, 1))
        return jnp.where(lane < 4 * air_x, low, pltpu.roll(sea_p, 4 * air_x, 1))

    def open_messages(lo_ref, hi_ref, air_ref, sea_ref):
        lo = jnp.where(gy == 0, 0.0, lo_ref[...])
        hi = jnp.where(gy == ny - 1, 0.0, hi_ref[...])
        lane = lane_of(lo)
        air = jnp.where(
            lax.rem(lane, 2 * air_x) < air_x, pltpu.roll(lo, 128 - air_x, 1), pltpu.roll(hi, air_x, 1)
        )
        air_ref[...] = jnp.concatenate([air, pltpu.roll(air, 128 - 2 * air_x, 1)], axis=0)
        lo = pltpu.roll(lo, 128 - 4 * air_x - sea_x, 1)
        hi = pltpu.roll(hi, 128 - 4 * air_x + sea_x, 1)
        sea_ref[...] = jnp.where(lane < sea_x, lo, hi)

    def packed_air(ref):
        p = jnp.zeros((128, 128), f32)
        for x in range(air_x):
            p = put_ends(p, ref[x], x, air_x + x)
        return p

    def packed_sea(ref):
        p = jnp.zeros((64, 128), f32)
        for x in range(sea_x):
            p = put_ends(p, ref[x], x, sea_x + x)
        return p

    def phase_mask():
        loaded_mask = mask_s[...].astype(f32)
        mf[...] = loaded_mask
        for x in range(sea_x):
            sv_s[x] = loaded_mask[x:x + 1, :] * sv_s[x]

    def phase_pack():
        mine[...] = message(packed_air(av_s), packed_sea(sv_s))

    def phase_matrices():
        wcat[...] = split_cat(wa_s[...])
        wcat_t[...] = split_cat(wa_s[...].T)
        ocat[...] = split_cat(wo_s[...])
        ocat_t[...] = split_cat(wo_s[...].T)

    row_blocks = 32 * nx

    def places(idx_s, cnt_s, dx):
        own = gx * 32 + lax.broadcasted_iota(jnp.int32, (4, 32), 1)
        rel = idx_s[...] - own
        d = jnp.where(rel == 0, 0.0, jnp.where((rel == 1) | (rel == 1 - row_blocks), 1.0, -1.0))
        block = lax.broadcasted_iota(jnp.int32, (128, 32), 0) // 4
        pick = jnp.where(block == lax.broadcasted_iota(jnp.int32, (128, 32), 1), 1.0, 0.0)
        count = cnt_s[...].astype(f32)
        for k in range(4):
            dk = jnp.where(count > k, d[k:k + 1, :], 2.0)
            dx[k] = jnp.broadcast_to(jnp.sum(pick * dk, axis=1, keepdims=True), (128, 128))

    def phase_places():
        places(fidx_s, fcnt_s, dx_f)
        places(sidx_s, scnt_s, dx_s)

    def air_first(x, west, east):
        v = av_s[x]
        at[x] = col(wcat[...], as_s[x] * (GAIN * (v + west + east + lane_shifts(v))))

    def sea_first(x, west, east):
        v = sv_s[x]
        s1[x] = v + (GAIN * mf[x:x + 1, :]) * (west + east + lane_shifts(v) - 4.0 * v)

    def phase_air_first():
        for x in range(1, last_a):
            air_first(x, av_s[x - 1], av_s[x + 1])

    def phase_sea_first():
        for x in range(1, last_o):
            sea_first(x, sv_s[x - 1], sv_s[x + 1])

    def phase_as_pack():
        as_p[...] = packed_air(as_s)

    def phase_air_outer():
        air_first(0, xl_a[...], av_s[1])
        air_first(last_a, av_s[last_a - 1], xr_a[...])

    def phase_fix():
        fix[...] = col(wcat[...], as_p[...] * (GAIN * halo_a[...]))

    def air_ends(ref, x, rows=slice(None)):
        return ref[rows, x:x + 1], ref[rows, air_x + x:air_x + x + 1]

    def sea_ends(ref, x, rows=slice(None)):
        return ref[rows, x:x + 1], ref[rows, sea_x + x:sea_x + x + 1]

    def phase_air_surface():
        for x in range(air_x):
            low = rounded(with_ends(at[x, 120:128, :], *air_ends(fix, x, slice(120, 128))))
            S_a[8 + 8 * x:16 + 8 * x, :] = jnp.where(half, pltpu.roll(low[:, 0:128], 4, 0), low[:, 128:256])

    def sea_finish(x, v, rows):
        lo, hi = sea_ends(halo_o, x, rows)
        return with_ends(v, (GAIN * mf[x:x + 1, 0:1]) * lo, (GAIN * mf[x:x + 1, -1:]) * hi)

    def sea_outer(rows):
        for x, west, east in ((0, xl_o, sv_s.at[1]), (last_o, sv_s.at[last_o - 1], xr_o)):
            v = sv_s[x, rows, :]
            s1[x, rows, :] = v + (GAIN * mf[x:x + 1, :]) * (
                west[rows, :] + east[rows, :] + lane_shifts(v) - 4.0 * v
            )

    def to_slabs(top):
        out = []
        for q in range(2):
            a, b = top[:, 256 * q:256 * q + 128], top[:, 256 * q + 128:256 * q + 256]
            out.append(jnp.where(half, a, pltpu.roll(b, 4, 0)))
        return jnp.concatenate(out, axis=0)

    def phase_sea_surface():
        sea_outer(slice(0, 8))
        for x in range(sea_x):
            top = sea_finish(x, s1[x, 0:8, :], slice(0, 8))
            S_o[8 + 16 * x:24 + 16 * x, :] = to_slabs(rounded(top))

    def phase_sea_outer():
        sea_outer(slice(8, 64))

    def send_rims(src_hi, src_lo, k):
        return start(
            remote(src_hi.at[128:136], src_hi.at[0:8], k, to_right),
            remote(src_lo.at[8:16], src_lo.at[136:144], k + 1, to_left),
        )

    def gather_rows(S, dx, L, r0, r1):
        s_m, s_0, s_p = S[4 + r0:4 + r1], S[8 + r0:8 + r1], S[12 + r0:12 + r1]
        for k in range(4):
            d = dx[k, r0:r1]
            L[r0:r1, 128 * k:128 * k + 128] = jnp.where(
                d == 0.0, s_0, jnp.where(d == -1.0, s_m, jnp.where(d == 1.0, s_p, 0.0))
            )

    def pair_tiles(T, p):
        return jnp.concatenate(
            [jnp.concatenate([T[2 * p + a, k] for k in range(4)], axis=1) for a in range(2)], axis=0
        )

    def forward_pair(L, T, out, p):
        r = lax.dot_general(
            L[8 * p:8 * p + 8, :].astype(bf16), pair_tiles(T, p), (((1,), (1,)), ((), ())),
            preferred_element_type=f32,
        )
        out[8 * p:8 * p + 8, :] = jnp.where(half, r[:, 0:128], r[:, 128:256])

    def back_pair(A, T, dx, C, p):
        a = A[8 * p:8 * p + 8, :]
        lhs = jnp.concatenate([jnp.where(half, a, 0.0), jnp.where(half, 0.0, a)], axis=1)
        r = jnp.dot(lhs.astype(bf16), pair_tiles(T, p), preferred_element_type=f32)
        sums = [jnp.zeros((8, 128), f32) for _ in range(3)]
        for k in range(4):
            d = dx[k, 8 * p:8 * p + 8, :]
            c = r[:, 128 * k:128 * k + 128]
            for n in range(3):
                sums[n] = sums[n] + jnp.where(d == n - 1.0, c, 0.0)
        for n in range(3):
            C[n, 8 + 8 * p:16 + 8 * p, :] = sums[n]

    def phase_forward_skin():
        gather_rows(S_o, dx_s, L_s, 8, 120)
        for p in range(1, 15):
            forward_pair(L_s, st_s, G, p)

    def phase_forward_flux():
        gather_rows(S_a, dx_f, L_f, 8, 120)
        for p in range(1, 15):
            forward_pair(L_f, ft_s, F, p)

    def phase_forward_rims():
        for r0 in (0, 120):
            gather_rows(S_a, dx_f, L_f, r0, r0 + 8)
            gather_rows(S_o, dx_s, L_s, r0, r0 + 8)
        for p in (0, 15):
            forward_pair(L_f, ft_s, F, p)
            forward_pair(L_s, st_s, G, p)

    def sea_top(ref, x):
        parts = []
        for q in range(2):
            slab = ref[16 * x + 8 * q:16 * x + 8 * q + 8, :]
            parts.append(jnp.where(half, slab, 0.0))
            parts.append(jnp.where(half, pltpu.roll(slab, 4, 0), 0.0))
        return jnp.concatenate(parts, axis=1)

    def sea_columns(x):
        m = mf[x:x + 1, :]
        one = sea_finish(x, s1[x], slice(None))
        two = jnp.concatenate([one[0:8] + m * sea_top(F, x), one[8:]], axis=0)
        three = col(ocat[...], ss_s[x] * two)
        back = m * (ss_s[x] * col(ocat_t[...], m * (sw_s[x] * three)))
        adj[x] = back
        A_f[16 * x:16 * x + 16, :] = to_slabs(rounded(back[0:8]))

    def phase_sea_columns_outer():
        sea_columns(0)
        sea_columns(last_o)

    def phase_sea_columns():
        for x in range(1, last_o):
            sea_columns(x)

    def air_low(ref, x):
        slab = ref[8 * x:8 * x + 8, :]
        return jnp.concatenate(
            [jnp.where(half, 0.0, pltpu.roll(slab, 4, 0)), jnp.where(half, 0.0, slab)], axis=1
        )

    def air_forcing(x):
        two = with_ends(at[x], *air_ends(fix, x))
        three = jnp.concatenate([two[0:120], two[120:128] + air_low(G, x)], axis=0)
        forcing = aw_s[x] * three
        at[x] = forcing
        low = rounded(forcing[120:128])
        A_s[8 * x:8 * x + 8, :] = jnp.where(half, pltpu.roll(low[:, 0:128], 4, 0), low[:, 128:256])

    def phase_air_forcing_outer():
        air_forcing(0)
        air_forcing(last_a)

    def phase_air_forcing():
        for x in range(1, last_a):
            air_forcing(x)

    def phase_air_pack():
        af_p[...] = packed_air(at)

    def phase_back_flux_rims():
        for p in (0, 1, 14, 15):
            back_pair(A_f, ft_s, dx_f, Cf, p)

    def phase_back_flux():
        for p in range(2, 14):
            back_pair(A_f, ft_s, dx_f, Cf, p)

    def phase_back_skin():
        for p in range(16):
            back_pair(A_s, st_s, dx_s, Cs, p)

    def own_terms(C, R, r0, r1):
        R[r0:r1, :] = C[1, r0 + 8:r1 + 8] + C[0, r0 + 12:r1 + 12] + C[2, r0 + 4:r1 + 4]

    def own_terms_ends(C, R):
        R[0:8, :] = C[1, 8:16] + C[0, 12:20] + jnp.where(half, 0.0, pltpu.roll(C[2, 8:16], 4, 0))
        R[120:128, :] = C[1, 128:136] + C[2, 124:132] + jnp.where(half, pltpu.roll(C[0, 128:136], 4, 0), 0.0)

    def air_lower(xs):
        p = af_p[120:128, :]
        for x in xs:
            low = at[x, 120:128, :] + air_low(R_f, x)
            at[x, 120:128, :] = low
            p = put_ends(p, low, x, air_x + x)
        af_p[120:128, :] = p

    def phase_own_outer():
        own_terms_ends(Cf, R_f)
        air_lower((0, last_a))
        own_l[...] = as_s[0] * col(wcat_t[...], at[0])
        own_r[...] = as_s[last_a] * col(wcat_t[...], at[last_a])

    def phase_air_lower():
        own_terms(Cf, R_f, 8, 120)
        air_lower(range(1, last_a))

    def phase_sea_upper():
        own_terms(Cs, R_s, 8, 120)
        own_terms_ends(Cs, R_s)
        for x in range(sea_x):
            adj[x, 0:8, :] = adj[x, 0:8, :] + mf[x:x + 1, :] * sea_top(R_s, x)
        top_l[...] = adj[0, 0:8, :]
        top_r[...] = adj[last_o, 0:8, :]

    zero_rows = jnp.zeros((120, 128), f32)

    def low_rows(slab, first):
        rows = pltpu.roll(slab, 4, 0) if first else slab
        return jnp.concatenate([zero_rows, jnp.where(half, 0.0, rows)], axis=0)

    def phase_beside():
        terms = jnp.concatenate([low_rows(Cf[0, 8:16], True), low_rows(Cf[2, 128:136], False)], axis=1)
        r = col(wcat_t[...], terms)
        as_l[...] = as_l[...] * r[:, :128]
        as_r[...] = as_r[...] * r[:, 128:]

    def phase_rims_arrived():
        at[0, 120:128, 0:128] = at[0, 120:128, 0:128] + jnp.where(half, 0.0, Cf[2, 0:8])
        at[last_a, 120:128, 128:] = at[last_a, 120:128, 128:] + jnp.where(half, 0.0, pltpu.roll(Cf[0, 136:144], 4, 0))
        first = jnp.where(half, pltpu.roll(Cs[2, 0:8], 4, 0), 0.0)
        adj[0, 0:8, 0:128] = adj[0, 0:8, 0:128] + mf[0:1, 0:128] * first
        final = jnp.where(half, Cs[0, 136:144], 0.0)
        adj[last_o, 0:8, -128:] = adj[last_o, 0:8, -128:] + mf[last_o:last_o + 1, -128:] * final

    def phase_diagonal():
        lo = jnp.where(gy == 0, 0.0, 1.0)
        hi = jnp.where(gy == ny - 1, 0.0, 1.0)
        lane = lane_of(zero_rows)[0:8]
        t_lo = lo * jnp.where(half, 0.0, pltpu.roll(df_lo[...], 4, 0))
        t_hi = hi * jnp.where(half, 0.0, df_hi[...])
        tile = jnp.where(lane == last_a, t_lo[:, 127:128], jnp.where(lane == air_x, t_hi[:, 0:1], 0.0))
        r = col(wcat_t[...], jnp.concatenate([zero_rows, tile], axis=0))
        scale = jnp.concatenate([from_lo2[:, 81:82], from_lo2[:, 83:84]], axis=0)
        scale_hi = jnp.concatenate([from_hi2[:, 80:81], from_hi2[:, 82:83]], axis=0)
        wide = lane_of(r)
        halo2_a[...] = halo2_a[...] + r * jnp.where(wide == last_a, scale, jnp.where(wide == air_x, scale_hi, 0.0))
        o_lo = lo * jnp.where(half, ds_lo[...], 0.0)
        o_hi = hi * jnp.where(half, pltpu.roll(ds_hi[...], 4, 0), 0.0)
        o_lo = o_lo[:, 127:128] * from_lo2[0:8, 85:86]
        o_hi = o_hi[:, 0:1] * from_hi2[0:8, 84:85]
        halo2_o[0:8, :] = halo2_o[0:8, :] + jnp.where(
            lane == last_o, o_lo, jnp.where(lane == sea_x, o_hi, 0.0)
        )

    def phase_pack_last():
        air_p = as_p[...] * col(wcat_t[...], af_p[...])
        m = message(air_p, packed_sea(adj))
        lane = lane_of(m)
        first, final = as_p[:, 0:1], as_p[:, air_x + last_a:air_x + last_a + 1]
        extra = (
            (80, first[:64]), (82, first[64:]), (81, final[:64]), (83, final[64:]),
            (84, mf[0:1, 0:1]), (85, mf[last_o:last_o + 1, -1:]),
        )
        for n, v in extra:
            m = jnp.where(lane == n, v, m)
        mine2[...] = m

    def air_upper(x):
        au[x] = as_s[x] * col(wcat_t[...], at[x])

    def phase_air_upper_outer():
        air_upper(0)
        air_upper(last_a)

    def phase_air_upper():
        for x in range(1, last_a):
            air_upper(x)

    def sea_last(x, west, east):
        z = adj[x]
        so[x] = z + (GAIN * mf[x:x + 1, :]) * (west + east + lane_shifts(z) - 4.0 * z)

    def air_last(x, west, east):
        v = au[x]
        ao[x] = GAIN * (v + west + east + lane_shifts(v))

    def phase_last():
        for x in range(2, last_o - 1):
            sea_last(x, adj[x - 1], adj[x + 1])
        for x in range(2, last_a - 1):
            air_last(x, au[x - 1], au[x + 1])

    def phase_last_next():
        for x in (1, last_o - 1):
            sea_last(x, adj[x - 1], adj[x + 1])
        for x in (1, last_a - 1):
            air_last(x, au[x - 1], au[x + 1])

    def last_ends(sea_xs, air_xs):
        for x in sea_xs:
            lo, hi = sea_ends(halo2_o, x)
            so[x] = with_ends(so[x], (GAIN * mf[x:x + 1, 0:1]) * lo, (GAIN * mf[x:x + 1, -1:]) * hi)
        for x in air_xs:
            lo, hi = air_ends(halo2_a, x)
            ao[x] = with_ends(ao[x], GAIN * lo, GAIN * hi)

    def last_outer():
        xl2_o[0:8, -128:] = xl2_o[0:8, -128:] + m_l[last_o:last_o + 1, :] * jnp.where(half, Cs[0, 8:16], 0.0)
        xr2_o[0:8, 0:128] = xr2_o[0:8, 0:128] + m_r[0:1, :] * jnp.where(half, pltpu.roll(Cs[2, 128:136], 4, 0), 0.0)
        xl2_a[:, 128:] = xl2_a[:, 128:] + as_l[...]
        xr2_a[:, 0:128] = xr2_a[:, 0:128] + as_r[...]
        sea_last(0, xl2_o[...], adj[1])
        sea_last(last_o, adj[last_o - 1], xr2_o[...])
        air_last(0, xl2_a[...], au[1])
        air_last(last_a, au[last_a - 1], xr2_a[...])
        last_ends((0, last_o), (0, last_a))

    pl.semaphore_wait(barrier, 6)
    halo_a1 = start(
        remote(av.at[:, last_a, :], xl_a, 0, to_right),
        remote(av.at[:, 0, :], xr_a, 1, to_left),
    )
    loaded(mask_s, 0)
    loaded(sv_s, 1)
    phase_mask()
    halo_o1 = start(
        remote(sv_s.at[last_o, 0:8], xl_o.at[0:8], 2, to_right),
        remote(sv_s.at[0, 0:8], xr_o.at[0:8], 3, to_left),
    )
    loaded(av_s, 2)
    phase_pack()
    halo_y1 = start(remote(mine, from_lo, 4, to_above), remote(mine, from_hi, 5, to_below))
    halo_o1_rest = start(
        remote(sv_s.at[last_o, 8:64], xl_o.at[8:64], 14, to_right),
        remote(sv_s.at[0, 8:64], xr_o.at[8:64], 15, to_left),
    )
    loaded(wa_s, 3)
    loaded(wo_s, 4)
    phase_matrices()
    loaded(fidx_s, 5)
    loaded(fcnt_s, 6)
    loaded(sidx_s, 7)
    loaded(scnt_s, 8)
    phase_places()
    phase_sea_first()
    loaded(as_s, 9)
    phase_air_first()
    phase_as_pack()

    wait(halo_y1)
    open_messages(from_lo, from_hi, halo_a, halo_o)
    phase_fix()
    wait(halo_o1)
    phase_sea_surface()
    rim_o = send_rims(S_o, S_o, 8)
    wait(halo_a1)
    phase_air_outer()
    phase_air_surface()
    rim_a = send_rims(S_a, S_a, 6)

    loaded(st_s, 11)
    phase_forward_skin()
    loaded(ft_s, 10)
    phase_forward_flux()
    beside = start(
        remote(asc.at[:, last_a, 128:256], as_l, 24, to_right),
        remote(asc.at[:, 0, 0:128], as_r, 25, to_left),
        remote(mf.at[:, mf.shape[1] - 128:], m_l, 26, to_right),
        remote(mf.at[:, 0:128], m_r, 27, to_left),
    )
    loaded(ss_s, 12)
    loaded(sw_s, 13)
    phase_sea_columns()
    loaded(aw_s, 14)
    phase_air_forcing()
    wait(rim_a)
    wait(rim_o)
    phase_forward_rims()
    wait(halo_o1_rest)
    phase_sea_outer()
    phase_sea_columns_outer()
    halo_o2_rest = start(
        remote(adj.at[last_o, 8:64], xl2_o.at[8:64], 16, to_right),
        remote(adj.at[0, 8:64], xr2_o.at[8:64], 17, to_left),
    )
    phase_air_forcing_outer()
    phase_back_flux_rims()
    rim_f = send_rims(Cf.at[2], Cf.at[0], 10)
    diagonal = start(
        remote(Cf.at[0, 8:16], df_lo, 28, to_left_above),
        remote(Cf.at[2, 128:136], df_hi, 29, to_right_below),
    )
    phase_air_pack()
    phase_own_outer()
    halo_a2 = start(remote(own_r, xl2_a, 18, to_right), remote(own_l, xr2_a, 19, to_left))
    phase_back_skin()
    rim_s = send_rims(Cs.at[2], Cs.at[0], 12)
    diagonal += start(
        remote(Cs.at[0, 8:16], ds_lo, 30, to_left_above),
        remote(Cs.at[2, 128:136], ds_hi, 31, to_right_below),
    )
    phase_sea_upper()
    halo_o2 = start(
        remote(top_r, xl2_o.at[0:8], 20, to_right),
        remote(top_l, xr2_o.at[0:8], 21, to_left),
    )
    phase_back_flux()
    phase_air_lower()
    phase_pack_last()
    halo_y2 = start(remote(mine2, from_lo2, 22, to_above), remote(mine2, from_hi2, 23, to_below))
    phase_air_upper()
    wait(beside)
    phase_beside()
    phase_last()
    wait(rim_f)
    wait(rim_s)
    phase_rims_arrived()
    phase_air_upper_outer()
    phase_last_next()
    wait(halo_y2)
    open_messages(from_lo2, from_hi2, halo2_a, halo2_o)
    wait(diagonal)
    phase_diagonal()
    last_ends(range(1, last_o), range(1, last_a))
    wait(halo_o2_rest)
    wait(halo_o2)
    wait(halo_a2)
    last_outer()


def deliver(a, o, aout, sout, sem):
    for x in range(a.shape[0]):
        pltpu.make_async_copy(a.at[x], aout.at[:, x, :], sem.at[0]).start()
    for x in range(o.shape[0]):
        pltpu.make_async_copy(o.at[x], sout.at[:, x, :], sem.at[1]).start()
    pltpu.make_async_copy(a, a, sem.at[0]).wait()
    pltpu.make_async_copy(o, o, sem.at[1]).wait()


def shards(*args, nx, ny):
    av, sv = args[0], args[1]
    args = [a.transpose(0, 2, 1) if n in (9, 12) else a for n, a in enumerate(args)]
    args = [pltpu.with_memory_space_constraint(a, pltpu.HBM) for a in args]
    levels, air_x, air_y = av.shape
    sea_levels, sea_x, sea_y = sv.shape
    V = pltpu.VMEM
    air = V((air_x, levels, air_y), f32)
    sea = V((sea_x, sea_levels, sea_y), f32)
    blk = V((128, 128), f32)
    ext = V((144, 128), f32)
    rowa, rowo, pack = V((levels, air_y), f32), V((sea_levels, sea_y), f32), V((64, 128), f32)
    tiles = V((32, 4, 128, 128), bf16)
    idx, cnt = V((4, 32), jnp.int32), V((1, 32), jnp.int32)
    wcat = V((2 * levels, 2 * levels), bf16)
    ocat = V((2 * sea_levels, 2 * sea_levels), bf16)
    dx = V((4, 128, 128), f32)
    cterm = V((3, 144, 128), f32)
    tile = V((8, 128), f32)
    dma = pltpu.SemaphoreType.DMA
    scratch = [
        air, sea, air, sea, air, sea, V((levels, levels), f32), V((sea_levels, sea_levels), f32),
        V((sea_x, sea_y), jnp.int32), idx, cnt, tiles, idx, cnt, tiles,
        wcat, wcat, ocat, ocat, V((sea_x, sea_y), f32),
        air, sea, sea, air,
        dx, dx, ext, ext, V((128, 512), f32), V((128, 512), f32), blk, blk, blk, blk, cterm, cterm, blk, blk,
        rowa, rowa, rowo, rowo, pack, pack, pack, blk, pack, blk, blk, blk,
        rowa, rowa, rowo, rowo, pack, pack, pack, blk, pack,
        rowa, rowa, V((8, sea_y), f32), V((8, sea_y), f32), blk, blk, tile, tile, tile, tile, tile, tile,
        dma((15,)), dma((32,)), dma((32,)),
    ]
    anywhere = pl.BlockSpec(memory_space=pl.ANY)
    outs = (jax.ShapeDtypeStruct(av.shape, f32), jax.ShapeDtypeStruct(sv.shape, f32))
    held = pl.pallas_call(
        functools.partial(kernel, nx, ny, air_x, sea_x),
        out_shape=(air, sea),
        in_specs=[pl.BlockSpec(memory_space=pltpu.HBM)] * 15,
        out_specs=[pl.BlockSpec(memory_space=pltpu.VMEM)] * 2,
        scratch_shapes=scratch,
        compiler_params=pltpu.CompilerParams(
            collective_id=0, has_side_effects=True, vmem_limit_bytes=44 * 1024 * 1024
        ),
        cost_estimate=pl.CostEstimate(flops=4_000_000_000, bytes_accessed=21_000_000, transcendentals=0),
    )(*args)
    return pl.pallas_call(
        deliver,
        out_shape=outs,
        in_specs=[anywhere] * 2,
        out_specs=[pl.BlockSpec(memory_space=pltpu.HBM)] * 2,
        scratch_shapes=[dma((2,))],
        compiler_params=pltpu.CompilerParams(vmem_limit_bytes=1024 * 1024),
    )(*held)


def solution(mesh):
    grid = P(None, "gx", "gy")
    index, count, tiles = P("gy", "gx", None), P("gy", "gx"), P("gy", "gx", None, None, None)
    return jax.shard_map(
        functools.partial(shards, nx=mesh.shape["gx"], ny=mesh.shape["gy"]),
        mesh=mesh,
        in_specs=(grid,) * 6 + (P(), P(), P("gx", "gy"), index, count, tiles, index, count, tiles),
        out_specs=(grid, grid),
        check_vma=False,
    )
```

```python
import functools

import jax
import jax.numpy as jnp
from jax import lax
from jax.experimental import pallas as pl
from jax.experimental.pallas import tpu as pltpu
from jax.sharding import PartitionSpec as P

GAIN = 0.2
MESH = pl.DeviceIdType.MESH
f32, bf16 = jnp.float32, jnp.bfloat16


def split_cat(w):
    hi = w.astype(bf16)
    lo = (w - hi.astype(f32)).astype(bf16)
    return jnp.concatenate(
        [jnp.concatenate([hi, hi], axis=1), jnp.concatenate([lo, lo], axis=1)], axis=0
    )


def col(cat, field):
    n = field.shape[0]
    hi = field.astype(bf16)
    lo = (field - hi.astype(f32)).astype(bf16)
    r = jnp.dot(cat, jnp.concatenate([hi, lo], axis=0), preferred_element_type=f32)
    return r[:n] + r[n:]


def rounded(v):
    return v.astype(bf16).astype(f32)


def lane_of(v):
    return lax.broadcasted_iota(jnp.int32, v.shape, 1)


def lane_shifts(v):
    n = v.shape[1]
    lane = lane_of(v)
    down = jnp.where(lane == 0, 0.0, pltpu.roll(v, 1, 1))
    up = jnp.where(lane == n - 1, 0.0, pltpu.roll(v, n - 1, 1))
    return down + up


def with_ends(v, lo, hi):
    head, tail = v[:, :128], v[:, -128:]
    lane = lane_of(head)
    head = jnp.where(lane == 0, head + lo, head)
    tail = jnp.where(lane == 127, tail + hi, tail)
    return jnp.concatenate([head, v[:, 128:-128], tail], axis=1) if v.shape[1] > 256 else jnp.concatenate(
        [head, tail], axis=1
    )


def put_ends(packed, field, lo, hi):
    lane = lane_of(packed)
    packed = jnp.where(lane == lo, field[:, 0:1], packed)
    return jnp.where(lane == hi, field[:, -1:], packed)


def kernel(
    nx, ny, air_x, sea_x,
    av, sv, asc, ssc, aw, sw, wa, wo, mask, fidx, fcnt, ftil, sidx, scnt, stil,
    ao, so,
    av_s, sv_s, as_s, ss_s, aw_s, sw_s, wa_s, wo_s, mask_s, fidx_s, fcnt_s, ft_s, sidx_s, scnt_s, st_s,
    wcat, wcat_t, ocat, ocat_t, mf,
    at, s1, adj, au,
    dx_f, dx_s, S_a, S_o, L_f, L_s, F, G, A_f, A_s, Cf, Cs, R_f, R_s,
    xl_a, xr_a, xl_o, xr_o, mine, from_lo, from_hi, halo_a, halo_o, as_p, fix, af_p,
    xl2_a, xr2_a, xl2_o, xr2_o, mine2, from_lo2, from_hi2, halo2_a, halo2_o,
    rim_lo, rim_hi, own_l, own_r, top_l, top_r, as_l, as_r, m_l, m_r, df_lo, df_hi, ds_lo, ds_hi,
    in_sem, send_sem, recv_sem,
):
    gx, gy = lax.axis_index("gx"), lax.axis_index("gy")
    right, left = lax.rem(gx + 1, nx), lax.rem(gx + nx - 1, nx)
    above, below = lax.rem(gy + 1, ny), lax.rem(gy + ny - 1, ny)
    to_right, to_left = (right, gy), (left, gy)
    to_above, to_below = (gx, above), (gx, below)
    to_left_above, to_right_below = (left, above), (right, below)
    last_a, last_o = air_x - 1, sea_x - 1

    def load_columns(src, dst, sem, count):
        for x in range(count):
            pltpu.make_async_copy(src.at[:, x, :], dst.at[x], in_sem.at[sem]).start()

    def loaded(dst, sem):
        pltpu.make_async_copy(dst, dst, in_sem.at[sem]).wait()

    def load(src, dst, sem):
        pltpu.make_async_copy(src, dst, in_sem.at[sem]).start()

    barrier = pltpu.get_barrier_semaphore()
    for device in (to_right, to_left, to_above, to_below, to_left_above, to_right_below):
        pl.semaphore_signal(barrier, inc=1, device_id=device, device_id_type=MESH)

    load(mask, mask_s, 0)
    load_columns(sv, sv_s, 1, sea_x)
    load_columns(av, av_s, 2, air_x)
    load(wa, wa_s, 3)
    load(wo, wo_s, 4)
    load(fidx.at[0], fidx_s, 5)
    load(fcnt, fcnt_s, 6)
    load(sidx.at[0], sidx_s, 7)
    load(scnt, scnt_s, 8)
    load_columns(asc, as_s, 9, air_x)
    load(ftil.at[0], ft_s, 10)
    load(stil.at[0], st_s, 11)
    load_columns(ssc, ss_s, 12, sea_x)
    load_columns(sw, sw_s, 13, sea_x)
    load_columns(aw, aw_s, 14, air_x)

    def remote(src, dst, k, device):
        return pltpu.make_async_remote_copy(
            src_ref=src, dst_ref=dst, send_sem=send_sem.at[k], recv_sem=recv_sem.at[k],
            device_id=device, device_id_type=MESH,
        )

    def start(*copies):
        for c in copies:
            c.start()
        return copies

    def wait(copies):
        for c in copies:
            c.wait()

    half = lax.broadcasted_iota(jnp.int32, (8, 128), 0) < 4

    def message(air_p, sea_p):
        lane = lane_of(sea_p)
        low = jnp.where(lane < 2 * air_x, air_p[:64], pltpu.roll(air_p[64:], 2 * air_x, 1))
        return jnp.where(lane < 4 * air_x, low, pltpu.roll(sea_p, 4 * air_x, 1))

    def open_messages(lo_ref, hi_ref, air_ref, sea_ref):
        lo = jnp.where(gy == 0, 0.0, lo_ref[...])
        hi = jnp.where(gy == ny - 1, 0.0, hi_ref[...])
        lane = lane_of(lo)
        air = jnp.where(
            lax.rem(lane, 2 * air_x) < air_x, pltpu.roll(lo, 128 - air_x, 1), pltpu.roll(hi, air_x, 1)
        )
        air_ref[...] = jnp.concatenate([air, pltpu.roll(air, 128 - 2 * air_x, 1)], axis=0)
        lo = pltpu.roll(lo, 128 - 4 * air_x - sea_x, 1)
        hi = pltpu.roll(hi, 128 - 4 * air_x + sea_x, 1)
        sea_ref[...] = jnp.where(lane < sea_x, lo, hi)

    def packed_air(ref):
        p = jnp.zeros((128, 128), f32)
        for x in range(air_x):
            p = put_ends(p, ref[x], x, air_x + x)
        return p

    def packed_sea(ref):
        p = jnp.zeros((64, 128), f32)
        for x in range(sea_x):
            p = put_ends(p, ref[x], x, sea_x + x)
        return p

    def phase_mask():
        loaded_mask = mask_s[...].astype(f32)
        mf[...] = loaded_mask
        for x in range(sea_x):
            sv_s[x] = loaded_mask[x:x + 1, :] * sv_s[x]

    def phase_pack():
        mine[...] = message(packed_air(av_s), packed_sea(sv_s))

    def phase_matrices():
        wcat[...] = split_cat(wa_s[...])
        wcat_t[...] = split_cat(wa_s[...].T)
        ocat[...] = split_cat(wo_s[...])
        ocat_t[...] = split_cat(wo_s[...].T)

    row_blocks = 32 * nx

    def places(idx_s, cnt_s, dx):
        own = gx * 32 + lax.broadcasted_iota(jnp.int32, (4, 32), 1)
        rel = idx_s[...] - own
        d = jnp.where(rel == 0, 0.0, jnp.where((rel == 1) | (rel == 1 - row_blocks), 1.0, -1.0))
        block = lax.broadcasted_iota(jnp.int32, (128, 32), 0) // 4
        pick = jnp.where(block == lax.broadcasted_iota(jnp.int32, (128, 32), 1), 1.0, 0.0)
        count = cnt_s[...].astype(f32)
        for k in range(4):
            dk = jnp.where(count > k, d[k:k + 1, :], 2.0)
            dx[k] = jnp.broadcast_to(jnp.sum(pick * dk, axis=1, keepdims=True), (128, 128))

    def phase_places():
        places(fidx_s, fcnt_s, dx_f)
        places(sidx_s, scnt_s, dx_s)

    def air_first(x, west, east):
        v = av_s[x]
        at[x] = col(wcat[...], as_s[x] * (GAIN * (v + west + east + lane_shifts(v))))

    def sea_first(x, west, east):
        v = sv_s[x]
        s1[x] = v + (GAIN * mf[x:x + 1, :]) * (west + east + lane_shifts(v) - 4.0 * v)

    def phase_air_first():
        for x in range(1, last_a):
            air_first(x, av_s[x - 1], av_s[x + 1])

    def phase_sea_first():
        for x in range(1, last_o):
            sea_first(x, sv_s[x - 1], sv_s[x + 1])

    def phase_as_pack():
        as_p[...] = packed_air(as_s)

    def outer_halves(first, final):
        fields = []
        for x, west, east, lanes in ((0, xl_a, av_s.at[1], first), (last_a, av_s.at[last_a - 1], xr_a, final)):
            v = av_s[x]
            near = v + lane_shifts(v)
            fields.append(as_s[x, :, lanes] * (GAIN * (near[:, lanes] + west[:, lanes] + east[:, lanes])))
        r = col(wcat[...], jnp.concatenate(fields, axis=1))
        at[0, :, first] = r[:, 0:128]
        at[last_a, :, final] = r[:, 128:256]

    low_half, high_half = slice(0, 128), slice(128, 256)

    def phase_air_ends():
        outer_halves(low_half, high_half)

    def phase_air_outer():
        outer_halves(high_half, low_half)

    def phase_fix():
        fix[...] = col(wcat[...], as_p[...] * (GAIN * halo_a[...]))

    def air_ends(ref, x, rows=slice(None)):
        return ref[rows, x:x + 1], ref[rows, air_x + x:air_x + x + 1]

    def sea_ends(ref, x, rows=slice(None)):
        return ref[rows, x:x + 1], ref[rows, sea_x + x:sea_x + x + 1]

    def phase_air_rims():
        lane = lane_of(fix[120:128, :])
        a = at[0, 120:128, 0:128] + jnp.where(lane == 0, fix[120:128, 0:1], 0.0)
        b = at[last_a, 120:128, 128:256] + jnp.where(lane == 127, fix[120:128, 2 * air_x - 1:2 * air_x], 0.0)
        rim_lo[...] = jnp.where(half, pltpu.roll(rounded(a), 4, 0), 0.0)
        rim_hi[...] = jnp.where(half, 0.0, rounded(b))

    def phase_air_surface():
        for x in range(air_x):
            low = rounded(with_ends(at[x, 120:128, :], *air_ends(fix, x, slice(120, 128))))
            S_a[8 + 8 * x:16 + 8 * x, :] = jnp.where(half, pltpu.roll(low[:, 0:128], 4, 0), low[:, 128:256])

    def sea_finish(x, v, rows):
        lo, hi = sea_ends(halo_o, x, rows)
        return with_ends(v, (GAIN * mf[x:x + 1, 0:1]) * lo, (GAIN * mf[x:x + 1, -1:]) * hi)

    def sea_outer(rows):
        for x, west, east in ((0, xl_o, sv_s.at[1]), (last_o, sv_s.at[last_o - 1], xr_o)):
            v = sv_s[x, rows, :]
            s1[x, rows, :] = v + (GAIN * mf[x:x + 1, :]) * (
                west[rows, :] + east[rows, :] + lane_shifts(v) - 4.0 * v
            )

    def to_slabs(top):
        out = []
        for q in range(2):
            a, b = top[:, 256 * q:256 * q + 128], top[:, 256 * q + 128:256 * q + 256]
            out.append(jnp.where(half, a, pltpu.roll(b, 4, 0)))
        return jnp.concatenate(out, axis=0)

    def phase_sea_surface():
        sea_outer(slice(0, 8))
        for x in range(sea_x):
            top = sea_finish(x, s1[x, 0:8, :], slice(0, 8))
            S_o[8 + 16 * x:24 + 16 * x, :] = to_slabs(rounded(top))

    def phase_sea_outer():
        sea_outer(slice(8, 64))

    def send_rims(src_hi, src_lo, k):
        return start(
            remote(src_hi.at[128:136], src_hi.at[0:8], k, to_right),
            remote(src_lo.at[8:16], src_lo.at[136:144], k + 1, to_left),
        )

    def gather_rows(S, dx, L, r0, r1):
        s_m, s_0, s_p = S[4 + r0:4 + r1], S[8 + r0:8 + r1], S[12 + r0:12 + r1]
        for k in range(4):
            d = dx[k, r0:r1]
            L[r0:r1, 128 * k:128 * k + 128] = jnp.where(
                d == 0.0, s_0, jnp.where(d == -1.0, s_m, jnp.where(d == 1.0, s_p, 0.0))
            )

    def pair_tiles(T, p):
        return jnp.concatenate(
            [jnp.concatenate([T[2 * p + a, k] for k in range(4)], axis=1) for a in range(2)], axis=0
        )

    def forward_pair(L, T, out, p):
        r = lax.dot_general(
            L[8 * p:8 * p + 8, :].astype(bf16), pair_tiles(T, p), (((1,), (1,)), ((), ())),
            preferred_element_type=f32,
        )
        out[8 * p:8 * p + 8, :] = jnp.where(half, r[:, 0:128], r[:, 128:256])

    def back_pair(A, T, dx, C, p):
        a = A[8 * p:8 * p + 8, :]
        lhs = jnp.concatenate([jnp.where(half, a, 0.0), jnp.where(half, 0.0, a)], axis=1)
        r = jnp.dot(lhs.astype(bf16), pair_tiles(T, p), preferred_element_type=f32)
        sums = [jnp.zeros((8, 128), f32) for _ in range(3)]
        for k in range(4):
            d = dx[k, 8 * p:8 * p + 8, :]
            c = r[:, 128 * k:128 * k + 128]
            for n in range(3):
                sums[n] = sums[n] + jnp.where(d == n - 1.0, c, 0.0)
        for n in range(3):
            C[n, 8 + 8 * p:16 + 8 * p, :] = sums[n]

    def phase_forward_skin():
        gather_rows(S_o, dx_s, L_s, 8, 120)
        for p in range(1, 15):
            forward_pair(L_s, st_s, G, p)

    def phase_forward_flux():
        gather_rows(S_a, dx_f, L_f, 8, 120)
        for p in range(1, 15):
            forward_pair(L_f, ft_s, F, p)

    def phase_forward_rims():
        for r0 in (0, 120):
            gather_rows(S_a, dx_f, L_f, r0, r0 + 8)
            gather_rows(S_o, dx_s, L_s, r0, r0 + 8)
        for p in (0, 15):
            forward_pair(L_f, ft_s, F, p)
            forward_pair(L_s, st_s, G, p)

    def sea_top(ref, x):
        parts = []
        for q in range(2):
            slab = ref[16 * x + 8 * q:16 * x + 8 * q + 8, :]
            parts.append(jnp.where(half, slab, 0.0))
            parts.append(jnp.where(half, pltpu.roll(slab, 4, 0), 0.0))
        return jnp.concatenate(parts, axis=1)

    def sea_columns(x):
        m = mf[x:x + 1, :]
        one = sea_finish(x, s1[x], slice(None))
        two = jnp.concatenate([one[0:8] + m * sea_top(F, x), one[8:]], axis=0)
        three = col(ocat[...], ss_s[x] * two)
        back = m * (ss_s[x] * col(ocat_t[...], m * (sw_s[x] * three)))
        adj[x] = back
        A_f[16 * x:16 * x + 16, :] = to_slabs(rounded(back[0:8]))

    def phase_sea_columns_outer():
        sea_columns(0)
        sea_columns(last_o)

    def phase_sea_columns():
        for x in range(1, last_o):
            sea_columns(x)

    def air_low(ref, x):
        slab = ref[8 * x:8 * x + 8, :]
        return jnp.concatenate(
            [jnp.where(half, 0.0, pltpu.roll(slab, 4, 0)), jnp.where(half, 0.0, slab)], axis=1
        )

    def air_forcing(x):
        two = with_ends(at[x], *air_ends(fix, x))
        three = jnp.concatenate([two[0:120], two[120:128] + air_low(G, x)], axis=0)
        forcing = aw_s[x] * three
        at[x] = forcing
        low = rounded(forcing[120:128])
        A_s[8 * x:8 * x + 8, :] = jnp.where(half, pltpu.roll(low[:, 0:128], 4, 0), low[:, 128:256])

    def phase_air_forcing_outer():
        air_forcing(0)
        air_forcing(last_a)

    def phase_air_forcing():
        for x in range(1, last_a):
            air_forcing(x)

    def phase_air_pack():
        p = jnp.zeros((128, 128), f32)
        for x in range(1, last_a):
            p = put_ends(p, at[x], x, air_x + x)
        af_p[...] = p

    def phase_air_pack_outer():
        p = put_ends(af_p[...], at[0], 0, air_x)
        af_p[...] = put_ends(p, at[last_a], last_a, air_x + last_a)

    def phase_back_flux_rims():
        for p in (0, 1, 14, 15):
            back_pair(A_f, ft_s, dx_f, Cf, p)

    def phase_back_flux():
        for p in range(2, 14):
            back_pair(A_f, ft_s, dx_f, Cf, p)

    def phase_back_skin():
        for p in range(16):
            back_pair(A_s, st_s, dx_s, Cs, p)

    def own_terms(C, R, r0, r1):
        R[r0:r1, :] = C[1, r0 + 8:r1 + 8] + C[0, r0 + 12:r1 + 12] + C[2, r0 + 4:r1 + 4]

    def own_terms_ends(C, R):
        R[0:8, :] = C[1, 8:16] + C[0, 12:20] + jnp.where(half, 0.0, pltpu.roll(C[2, 8:16], 4, 0))
        R[120:128, :] = C[1, 128:136] + C[2, 124:132] + jnp.where(half, pltpu.roll(C[0, 128:136], 4, 0), 0.0)

    def air_lower(xs):
        p = af_p[120:128, :]
        for x in xs:
            low = at[x, 120:128, :] + air_low(R_f, x)
            at[x, 120:128, :] = low
            p = put_ends(p, low, x, air_x + x)
        af_p[120:128, :] = p

    def phase_own_outer():
        own_terms_ends(Cf, R_f)
        air_lower((0, last_a))
        own_l[...] = as_s[0] * col(wcat_t[...], at[0])
        own_r[...] = as_s[last_a] * col(wcat_t[...], at[last_a])

    def phase_air_lower():
        own_terms(Cf, R_f, 8, 120)
        air_lower(range(1, last_a))

    def phase_sea_upper():
        own_terms(Cs, R_s, 8, 120)
        own_terms_ends(Cs, R_s)
        for x in range(sea_x):
            adj[x, 0:8, :] = adj[x, 0:8, :] + mf[x:x + 1, :] * sea_top(R_s, x)
        top_l[...] = adj[0, 0:8, :]
        top_r[...] = adj[last_o, 0:8, :]

    zero_rows = jnp.zeros((120, 128), f32)

    def low_rows(slab, first):
        rows = pltpu.roll(slab, 4, 0) if first else slab
        return jnp.concatenate([zero_rows, jnp.where(half, 0.0, rows)], axis=0)

    def phase_beside():
        terms = jnp.concatenate([low_rows(Cf[0, 8:16], True), low_rows(Cf[2, 128:136], False)], axis=1)
        r = col(wcat_t[...], terms)
        as_l[...] = as_l[...] * r[:, :128]
        as_r[...] = as_r[...] * r[:, 128:]

    def phase_rims_arrived():
        at[0, 120:128, 0:128] = at[0, 120:128, 0:128] + jnp.where(half, 0.0, Cf[2, 0:8])
        at[last_a, 120:128, 128:] = at[last_a, 120:128, 128:] + jnp.where(half, 0.0, pltpu.roll(Cf[0, 136:144], 4, 0))
        first = jnp.where(half, pltpu.roll(Cs[2, 0:8], 4, 0), 0.0)
        adj[0, 0:8, 0:128] = adj[0, 0:8, 0:128] + mf[0:1, 0:128] * first
        final = jnp.where(half, Cs[0, 136:144], 0.0)
        adj[last_o, 0:8, -128:] = adj[last_o, 0:8, -128:] + mf[last_o:last_o + 1, -128:] * final

    def phase_diagonal():
        lo = jnp.where(gy == 0, 0.0, 1.0)
        hi = jnp.where(gy == ny - 1, 0.0, 1.0)
        lane = lane_of(zero_rows)[0:8]
        t_lo = lo * jnp.where(half, 0.0, pltpu.roll(df_lo[...], 4, 0))
        t_hi = hi * jnp.where(half, 0.0, df_hi[...])
        tile = jnp.where(lane == last_a, t_lo[:, 127:128], jnp.where(lane == air_x, t_hi[:, 0:1], 0.0))
        r = col(wcat_t[...], jnp.concatenate([zero_rows, tile], axis=0))
        scale = jnp.concatenate([from_lo2[:, 81:82], from_lo2[:, 83:84]], axis=0)
        scale_hi = jnp.concatenate([from_hi2[:, 80:81], from_hi2[:, 82:83]], axis=0)
        wide = lane_of(r)
        halo2_a[...] = halo2_a[...] + r * jnp.where(wide == last_a, scale, jnp.where(wide == air_x, scale_hi, 0.0))
        o_lo = lo * jnp.where(half, ds_lo[...], 0.0)
        o_hi = hi * jnp.where(half, pltpu.roll(ds_hi[...], 4, 0), 0.0)
        o_lo = o_lo[:, 127:128] * from_lo2[0:8, 85:86]
        o_hi = o_hi[:, 0:1] * from_hi2[0:8, 84:85]
        halo2_o[0:8, :] = halo2_o[0:8, :] + jnp.where(
            lane == last_o, o_lo, jnp.where(lane == sea_x, o_hi, 0.0)
        )

    def phase_pack_last():
        air_p = as_p[...] * col(wcat_t[...], af_p[...])
        m = message(air_p, packed_sea(adj))
        lane = lane_of(m)
        first, final = as_p[:, 0:1], as_p[:, air_x + last_a:air_x + last_a + 1]
        extra = (
            (80, first[:64]), (82, first[64:]), (81, final[:64]), (83, final[64:]),
            (84, mf[0:1, 0:1]), (85, mf[last_o:last_o + 1, -1:]),
        )
        for n, v in extra:
            m = jnp.where(lane == n, v, m)
        mine2[...] = m

    def air_upper(x):
        au[x] = as_s[x] * col(wcat_t[...], at[x])

    def phase_air_upper_outer():
        air_upper(0)
        air_upper(last_a)

    def phase_air_upper():
        for x in range(1, last_a):
            air_upper(x)

    def sea_last(x, west, east):
        z = adj[x]
        so[x] = z + (GAIN * mf[x:x + 1, :]) * (west + east + lane_shifts(z) - 4.0 * z)

    def air_last(x, west, east):
        v = au[x]
        ao[x] = GAIN * (v + west + east + lane_shifts(v))

    def phase_last():
        for x in range(2, last_o - 1):
            sea_last(x, adj[x - 1], adj[x + 1])
        for x in range(2, last_a - 1):
            air_last(x, au[x - 1], au[x + 1])

    def phase_last_next():
        for x in (1, last_o - 1):
            sea_last(x, adj[x - 1], adj[x + 1])
        for x in (1, last_a - 1):
            air_last(x, au[x - 1], au[x + 1])

    def last_ends(sea_xs, air_xs):
        for x in sea_xs:
            lo, hi = sea_ends(halo2_o, x)
            so[x] = with_ends(so[x], (GAIN * mf[x:x + 1, 0:1]) * lo, (GAIN * mf[x:x + 1, -1:]) * hi)
        for x in air_xs:
            lo, hi = air_ends(halo2_a, x)
            ao[x] = with_ends(ao[x], GAIN * lo, GAIN * hi)

    def last_outer():
        xl2_o[0:8, -128:] = xl2_o[0:8, -128:] + m_l[last_o:last_o + 1, :] * jnp.where(half, Cs[0, 8:16], 0.0)
        xr2_o[0:8, 0:128] = xr2_o[0:8, 0:128] + m_r[0:1, :] * jnp.where(half, pltpu.roll(Cs[2, 128:136], 4, 0), 0.0)
        xl2_a[:, 128:] = xl2_a[:, 128:] + as_l[...]
        xr2_a[:, 0:128] = xr2_a[:, 0:128] + as_r[...]
        sea_last(0, xl2_o[...], adj[1])
        sea_last(last_o, adj[last_o - 1], xr2_o[...])
        air_last(0, xl2_a[...], au[1])
        air_last(last_a, au[last_a - 1], xr2_a[...])
        last_ends((0, last_o), (0, last_a))

    pl.semaphore_wait(barrier, 6)
    halo_a1 = start(
        remote(av.at[:, last_a, 0:128], xl_a.at[:, 0:128], 0, to_right),
        remote(av.at[:, 0, 128:256], xr_a.at[:, 128:256], 1, to_left),
    )
    halo_a1_rest = start(
        remote(av.at[:, last_a, 128:256], xl_a.at[:, 128:256], 32, to_right),
        remote(av.at[:, 0, 0:128], xr_a.at[:, 0:128], 33, to_left),
    )
    loaded(mask_s, 0)
    loaded(sv_s, 1)
    phase_mask()
    halo_o1 = start(
        remote(sv_s.at[last_o, 0:8], xl_o.at[0:8], 2, to_right),
        remote(sv_s.at[0, 0:8], xr_o.at[0:8], 3, to_left),
    )
    loaded(av_s, 2)
    phase_pack()
    halo_y1 = start(remote(mine, from_lo, 4, to_above), remote(mine, from_hi, 5, to_below))
    halo_o1_rest = start(
        remote(sv_s.at[last_o, 8:64], xl_o.at[8:64], 14, to_right),
        remote(sv_s.at[0, 8:64], xr_o.at[8:64], 15, to_left),
    )
    loaded(wa_s, 3)
    loaded(wo_s, 4)
    phase_matrices()
    loaded(fidx_s, 5)
    loaded(fcnt_s, 6)
    loaded(sidx_s, 7)
    loaded(scnt_s, 8)
    phase_places()
    phase_sea_first()
    loaded(as_s, 9)
    phase_air_first()
    phase_as_pack()

    wait(halo_y1)
    open_messages(from_lo, from_hi, halo_a, halo_o)
    phase_fix()
    wait(halo_a1)
    phase_air_ends()
    phase_air_rims()
    rim_a = start(
        remote(rim_hi, S_a.at[0:8], 6, to_right),
        remote(rim_lo, S_a.at[136:144], 7, to_left),
    )
    wait(halo_o1)
    phase_sea_surface()
    rim_o = send_rims(S_o, S_o, 8)
    wait(halo_a1_rest)
    phase_air_outer()
    phase_air_surface()

    loaded(st_s, 11)
    phase_forward_skin()
    loaded(ft_s, 10)
    phase_forward_flux()
    beside = start(
        remote(asc.at[:, last_a, 128:256], as_l, 24, to_right),
        remote(asc.at[:, 0, 0:128], as_r, 25, to_left),
        remote(mf.at[:, mf.shape[1] - 128:], m_l, 26, to_right),
        remote(mf.at[:, 0:128], m_r, 27, to_left),
    )
    loaded(ss_s, 12)
    loaded(sw_s, 13)
    phase_sea_columns()
    loaded(aw_s, 14)
    phase_air_forcing()
    phase_air_pack()
    wait(halo_o1_rest)
    phase_sea_outer()
    wait(rim_a)
    wait(rim_o)
    phase_forward_rims()
    phase_sea_columns_outer()
    halo_o2_rest = start(
        remote(adj.at[last_o, 8:64], xl2_o.at[8:64], 16, to_right),
        remote(adj.at[0, 8:64], xr2_o.at[8:64], 17, to_left),
    )
    phase_air_forcing_outer()
    phase_back_flux_rims()
    rim_f = send_rims(Cf.at[2], Cf.at[0], 10)
    diagonal = start(
        remote(Cf.at[0, 8:16], df_lo, 28, to_left_above),
        remote(Cf.at[2, 128:136], df_hi, 29, to_right_below),
    )
    phase_air_pack_outer()
    phase_own_outer()
    halo_a2 = start(remote(own_r, xl2_a, 18, to_right), remote(own_l, xr2_a, 19, to_left))
    phase_back_skin()
    rim_s = send_rims(Cs.at[2], Cs.at[0], 12)
    diagonal += start(
        remote(Cs.at[0, 8:16], ds_lo, 30, to_left_above),
        remote(Cs.at[2, 128:136], ds_hi, 31, to_right_below),
    )
    phase_sea_upper()
    halo_o2 = start(
        remote(top_r, xl2_o.at[0:8], 20, to_right),
        remote(top_l, xr2_o.at[0:8], 21, to_left),
    )
    phase_back_flux()
    phase_air_lower()
    phase_pack_last()
    halo_y2 = start(remote(mine2, from_lo2, 22, to_above), remote(mine2, from_hi2, 23, to_below))
    phase_air_upper()
    wait(beside)
    phase_beside()
    phase_last()
    wait(rim_f)
    wait(rim_s)
    phase_rims_arrived()
    phase_air_upper_outer()
    phase_last_next()
    wait(halo_y2)
    open_messages(from_lo2, from_hi2, halo2_a, halo2_o)
    wait(diagonal)
    phase_diagonal()
    last_ends(range(1, last_o), range(1, last_a))
    wait(halo_o2_rest)
    wait(halo_o2)
    wait(halo_a2)
    last_outer()


def deliver(a, o, aout, sout, sem):
    for x in range(a.shape[0]):
        pltpu.make_async_copy(a.at[x], aout.at[:, x, :], sem.at[0]).start()
    for x in range(o.shape[0]):
        pltpu.make_async_copy(o.at[x], sout.at[:, x, :], sem.at[1]).start()
    pltpu.make_async_copy(a, a, sem.at[0]).wait()
    pltpu.make_async_copy(o, o, sem.at[1]).wait()


def shards(*args, nx, ny):
    av, sv = args[0], args[1]
    args = [a.transpose(0, 2, 1) if n in (9, 12) else a for n, a in enumerate(args)]
    args = [pltpu.with_memory_space_constraint(a, pltpu.HBM) for a in args]
    levels, air_x, air_y = av.shape
    sea_levels, sea_x, sea_y = sv.shape
    V = pltpu.VMEM
    air = V((air_x, levels, air_y), f32)
    sea = V((sea_x, sea_levels, sea_y), f32)
    blk = V((128, 128), f32)
    ext = V((144, 128), f32)
    rowa, rowo, pack = V((levels, air_y), f32), V((sea_levels, sea_y), f32), V((64, 128), f32)
    tiles = V((32, 4, 128, 128), bf16)
    idx, cnt = V((4, 32), jnp.int32), V((1, 32), jnp.int32)
    wcat = V((2 * levels, 2 * levels), bf16)
    ocat = V((2 * sea_levels, 2 * sea_levels), bf16)
    dx = V((4, 128, 128), f32)
    cterm = V((3, 144, 128), f32)
    tile = V((8, 128), f32)
    dma = pltpu.SemaphoreType.DMA
    scratch = [
        air, sea, air, sea, air, sea, V((levels, levels), f32), V((sea_levels, sea_levels), f32),
        V((sea_x, sea_y), jnp.int32), idx, cnt, tiles, idx, cnt, tiles,
        wcat, wcat, ocat, ocat, V((sea_x, sea_y), f32),
        air, sea, sea, air,
        dx, dx, ext, ext, V((128, 512), f32), V((128, 512), f32), blk, blk, blk, blk, cterm, cterm, blk, blk,
        rowa, rowa, rowo, rowo, pack, pack, pack, blk, pack, blk, blk, blk,
        rowa, rowa, rowo, rowo, pack, pack, pack, blk, pack,
        tile, tile, rowa, rowa, V((8, sea_y), f32), V((8, sea_y), f32), blk, blk, tile, tile, tile, tile, tile, tile,
        dma((15,)), dma((34,)), dma((34,)),
    ]
    anywhere = pl.BlockSpec(memory_space=pl.ANY)
    outs = (jax.ShapeDtypeStruct(av.shape, f32), jax.ShapeDtypeStruct(sv.shape, f32))
    held = pl.pallas_call(
        functools.partial(kernel, nx, ny, air_x, sea_x),
        out_shape=(air, sea),
        in_specs=[pl.BlockSpec(memory_space=pltpu.HBM)] * 15,
        out_specs=[pl.BlockSpec(memory_space=pltpu.VMEM)] * 2,
        scratch_shapes=scratch,
        compiler_params=pltpu.CompilerParams(
            collective_id=0, has_side_effects=True, vmem_limit_bytes=44 * 1024 * 1024
        ),
        cost_estimate=pl.CostEstimate(flops=4_000_000_000, bytes_accessed=21_000_000, transcendentals=0),
    )(*args)
    return pl.pallas_call(
        deliver,
        out_shape=outs,
        in_specs=[anywhere] * 2,
        out_specs=[pl.BlockSpec(memory_space=pltpu.HBM)] * 2,
        scratch_shapes=[dma((2,))],
        compiler_params=pltpu.CompilerParams(vmem_limit_bytes=1024 * 1024),
    )(*held)


def solution(mesh):
    grid = P(None, "gx", "gy")
    index, count, tiles = P("gy", "gx", None), P("gy", "gx"), P("gy", "gx", None, None, None)
    return jax.shard_map(
        functools.partial(shards, nx=mesh.shape["gx"], ny=mesh.shape["gy"]),
        mesh=mesh,
        in_specs=(grid,) * 6 + (P(), P(), P("gx", "gy"), index, count, tiles, index, count, tiles),
        out_specs=(grid, grid),
        check_vma=False,
    )
```
